128 devices in a mesh: group: 4 (over x), dev: 32 (over z, y, core).
Axes of the slice: x: 4, y: 4, z: 4, core: 2. Of those that a mesh axis runs over, the one named last changes fastest.
Arguments:
- node_features: bfloat16 [196608, 512], P(('group', 'dev')), may hold values from -8 to 8
- virtual_features: bfloat16 [16, 512], replicated, may hold values from -6 to 6
- w_qkv: bfloat16 [512, 1536], replicated, may hold values from -0.25 to 0.25
- output_weight: bfloat16 [512, 512], replicated, may hold values from -2 to 2
- block_home: int32 [1536], replicated, may hold values from 0 to 1535, as said below
- local_blocks: int32 [1536, 3], P(('group', 'dev')), may hold values from 0 to 1535, as said below
- expander_blocks: int32 [1536, 4], replicated, may hold values from 0 to 1535, as said below
- key_live: int32 [1536, 7], P(('group', 'dev')), may hold values from 16 to 128
- out_grad: bfloat16 [196608, 512], P(('group', 'dev')), may hold values from -6 to 6
Outputs:
- mixed: bfloat16 [196608, 512], P(('group', 'dev'))
- node_grad: bfloat16 [196608, 512], P(('group', 'dev'))
The draws below stay inside these ranges and needn't reach their ends.
Inputs may be any that keep to these rules, and one draw needn't show every extreme that they name: `block_home`: a permutation of the graph blocks; storage positions p * 12 to (p + 1) * 12 - 1 lie on index p of group+dev. `local_blocks`: row b names the block stored at b and two other blocks stored within b - 2 to b + 2. `expander_blocks`: the rows of one device name only blocks stored on other devices, at most 1 entries of them stored on any single device, and exactly 1 on some device.
All inputs are finite; a program needn't handle non-finite values.
Results may differ from the reference program's by a relative error of at most 0.024.
Values may be sent and summed in bfloat16 or wider, within the bound.
No kernel may reach another device: no remote copies, remote signals or barrier semaphores. Data moves between devices by JAX's collectives and lax.ppermute only.
A program may use at most 256 MiB of HBM per device.

```python
import jax
import jax.numpy as jnp
from jax import lax

D = 512
HEADS = 8
BLOCK = 128
LOCD = 3
EXPD = 4
VIRT = 16
BLK_DEV = 12
NB = 1536
NODES = 196608


def block_layout(key):
    home = jax.random.permutation(jax.random.fold_in(key, 101), NB).astype(jnp.int32)
    inverse = jnp.argsort(home).astype(jnp.int32)
    return (home, inverse)


def draw_block_home(key, part):
    home, inverse = block_layout(key)
    return home


def draw_local_blocks(key, part):
    home, inverse = block_layout(key)
    key = jax.random.fold_in(key, 2)
    position = jnp.arange(NB, dtype=jnp.int32)[:, None]
    offsets = jnp.array([-2, -1, 1, 2], dtype=jnp.int32)[None, :]
    target = position + offsets
    valid = (target >= 0) & (target < NB)
    score = jax.random.randint(key, (NB, 4), 0, 1000, dtype=jnp.int32) * 4 + jnp.arange(4, dtype=jnp.int32)[None, :]
    score = jnp.where(valid, score, -1)
    best, picks = lax.top_k(score, 2)
    chosen = jnp.take_along_axis(target, picks, axis=1)
    stored = jnp.concatenate([position, chosen], axis=1)
    return inverse[stored].astype(jnp.int32)


def draw_expander_blocks(key, part):
    home, inverse = block_layout(key)
    key = jax.random.fold_in(key, 3)
    devices = NB // BLK_DEV
    count = BLK_DEV * EXPD
    score = jax.random.randint(jax.random.fold_in(key, 1), (devices, devices - 1), 0, 1 << 20, dtype=jnp.int32)
    score = score * devices + jnp.arange(devices - 1, dtype=jnp.int32)[None, :]
    order = jnp.argsort(score, axis=1).astype(jnp.int32)
    pick = jnp.arange(count, dtype=jnp.int32) % (devices - 1)
    owner = (jnp.arange(devices, dtype=jnp.int32)[:, None] + 1 + order[:, pick]) % devices
    inner = jax.random.randint(jax.random.fold_in(key, 2), (devices, count), 0, BLK_DEV, dtype=jnp.int32)
    stored = (owner * BLK_DEV + inner).reshape(NB, EXPD)
    return inverse[stored].astype(jnp.int32)


def draw_node_features(key, part):
    key = jax.random.fold_in(key, 4)
    values = jnp.clip(jax.random.normal(jax.random.fold_in(key, 7), (NODES, D), jnp.float32), -6.0, 6.0)
    return values.astype(jnp.bfloat16)


def plant(values, key, least, largest):
    index_at = [jax.random.randint(jax.random.fold_in(key, axis), (), 0, length) for axis, length in enumerate(values.shape)]
    main_axis = values.shape.index(max(values.shape))
    next_to = index_at[:main_axis] + [(index_at[main_axis] + 1) % values.shape[main_axis]] + index_at[main_axis + 1:]
    return values.at[tuple(index_at)].set(least).at[tuple(next_to)].set(largest)


def shard_levels(own_key, shape, pieces, smallest, high):
    gain = 1.0
    for dim, blocks in pieces:
        draws = jax.random.uniform(jax.random.fold_in(jax.random.fold_in(own_key, 6), dim), (blocks,), jnp.float32, smallest / len(pieces), high / len(pieces))
        gain = gain * jnp.repeat(jnp.exp(draws), shape[dim] // blocks).reshape((-1,) + (1,) * (len(shape) - 1 - dim))
    return gain


def centred(key, dims, scale, bound, cuts=(), kind=jnp.bfloat16):
    result = jax.random.normal(key, dims, jnp.float32) * scale
    if len(cuts) > 0:
        result = shard_levels(key, dims, cuts, -0.22, 0.18) * result
    return jnp.clip(result, min=-bound, max=bound).astype(kind)


def setup_inputs(seed: int = 0) -> dict:
    streams_of = jax.random.split(jax.random.key(seed), 10)
    node_features = draw_node_features(jax.random.fold_in(streams_of[9], 71), 0)
    virtual_features = centred(streams_of[1], (VIRT, D), 1.0, 6.0)
    w_qkv = centred(streams_of[2], (D, 3 * D), D ** -0.5, 0.25)
    output_weight = centred(streams_of[3], (D, D), (D // 64) ** -0.5, 2.0)
    block_home = draw_block_home(jax.random.fold_in(streams_of[9], 71), 0)
    local_blocks = draw_local_blocks(jax.random.fold_in(streams_of[9], 71), 0)
    expander_blocks = draw_expander_blocks(jax.random.fold_in(streams_of[9], 71), 0)
    key_live = plant(jax.random.randint(streams_of[7], (NB, LOCD + EXPD), BLOCK // 8, BLOCK + 1), jax.random.fold_in(streams_of[7], 1), BLOCK // 8, BLOCK).astype(jnp.int32)
    out_grad = centred(streams_of[8], (NODES, D), 1.0, 6.0, ((0, 128),))
    return dict(node_features=node_features, virtual_features=virtual_features, w_qkv=w_qkv, output_weight=output_weight, block_home=block_home, local_blocks=local_blocks, expander_blocks=expander_blocks, key_live=key_live, out_grad=out_grad)


def rounded_retain(value):
    return lax.optimization_barrier(value.astype(jnp.bfloat16)).astype(jnp.float32)


def block_math(query, keys, virtual_kv, live, upstream_gradient, output_weight):
    count, lists, rows, double = keys.shape
    width = double // 2
    head_dim = width // HEADS
    scale = head_dim ** -0.5
    flat = keys.reshape(count, lists * rows, double)
    extra = jnp.broadcast_to(virtual_kv[None], (count, virtual_kv.shape[0], double))
    every = jnp.concatenate([flat, extra], axis=1).astype(jnp.float32)
    total_keys = every.shape[1]
    key_heads = every[:, :, :width].reshape(count, total_keys, HEADS, head_dim)
    val_heads = every[:, :, width:].reshape(count, total_keys, HEADS, head_dim)
    query_heads = query.astype(jnp.float32).reshape(count, rows, HEADS, head_dim)
    scores = jnp.einsum('nihe,njhe->nhij', query_heads, key_heads) * scale
    open_slot = (jnp.arange(rows, dtype=jnp.int32)[None, None, :] < live[:, :, None]).reshape(count, lists * rows)
    opened = jnp.concatenate([open_slot, jnp.ones((count, virtual_kv.shape[0]), dtype=bool)], axis=1)
    mask = opened[:, None, None, :]
    scores = jnp.where(mask, scores, -1e30)
    top = jnp.max(scores, axis=-1, keepdims=True)
    weights = jnp.exp(scores - top) * mask.astype(jnp.float32)
    probs = weights / jnp.sum(weights, axis=-1, keepdims=True)
    probs_b = rounded_retain(probs)
    attended_values = rounded_retain(jnp.einsum('nhij,njhe->nihe', probs_b, val_heads).reshape(count, rows, width))
    mixed = jnp.einsum('tbk,kr->tbr', attended_values, output_weight.astype(jnp.float32)).astype(jnp.bfloat16)
    attended_gradient = rounded_retain(jnp.einsum('asg,cg->asc', upstream_gradient.astype(jnp.float32), output_weight.astype(jnp.float32)))
    d_heads = attended_gradient.reshape(count, rows, HEADS, head_dim)
    d_probs = jnp.einsum('nihe,njhe->nhij', d_heads, val_heads)
    delta = jnp.einsum('nihe,nihe->nhi', d_heads, attended_values.reshape(count, rows, HEADS, head_dim))
    d_scores = rounded_retain(probs * (d_probs - delta[..., None]) * scale)
    d_query = jnp.einsum('nhij,njhe->nihe', d_scores, key_heads).reshape(count, rows, width).astype(jnp.bfloat16)
    d_key = jnp.einsum('nhij,nihe->njhe', d_scores, query_heads)[:, :lists * rows]
    d_val = jnp.einsum('nhij,nihe->njhe', probs_b, d_heads)[:, :lists * rows]
    key_grads = jnp.concatenate([d_key.reshape(count, lists, rows, width), d_val.reshape(count, lists, rows, width)], axis=-1)
    return mixed, d_query, key_grads


def reference(node_features, virtual_features, w_qkv, output_weight, block_home, local_blocks, expander_blocks, key_live, out_grad):
    width = node_features.shape[1]
    qkv = jnp.dot(node_features, w_qkv, preferred_element_type=jnp.float32).astype(jnp.bfloat16)
    qkv = qkv.reshape(NB, BLOCK, 3 * width)
    queries = qkv[:, :, :width]
    keyvals = qkv[:, :, width:]
    w_kv = w_qkv[:, width:]
    virtual_kv = jnp.dot(virtual_features, w_kv, preferred_element_type=jnp.float32).astype(jnp.bfloat16)
    local_at = block_home[local_blocks].astype(jnp.int32)
    far_at = block_home[expander_blocks].astype(jnp.int32)
    grads = out_grad.reshape(NB, BLOCK, width)

    def one_block(inputs):
        query, near_at, away_at, live, upstream_gradient = inputs
        keys = jnp.concatenate([keyvals[near_at], keyvals[away_at]], axis=0)[None]
        mixed, d_query, key_grads = block_math(query[None], keys, virtual_kv, live[None], upstream_gradient[None], output_weight)
        away = key_grads[0, LOCD:].astype(jnp.bfloat16).reshape(EXPD * BLOCK, 2 * width)
        far_term = jnp.dot(away, w_kv.T, preferred_element_type=jnp.float32).astype(jnp.bfloat16)
        return mixed[0], d_query[0], key_grads[0, :LOCD], far_term.reshape(EXPD, BLOCK, width)

    mixed, d_query, near_grads, far_terms = lax.map(one_block, (queries, local_at, far_at, key_live, grads))
    near_sum = jax.ops.segment_sum(near_grads.reshape(NB * LOCD, BLOCK, 2 * width), local_at.reshape(-1), num_segments=NB)
    far_sum = jax.ops.segment_sum(far_terms.reshape(NB * EXPD, BLOCK, width).astype(jnp.float32), far_at.reshape(-1), num_segments=NB)
    stacked = jnp.concatenate([d_query, near_sum.astype(jnp.bfloat16)], axis=2).reshape(NODES, 3 * width)
    node_grad = jnp.dot(stacked, w_qkv.T, preferred_element_type=jnp.float32) + far_sum.reshape(NODES, width)
    return mixed.reshape(NODES, width), node_grad.astype(jnp.bfloat16)
```

```python
import jax
import jax.numpy as jnp
from jax import lax
from jax.experimental import pallas as pl
from jax.experimental.pallas import tpu as pltpu
from jax.sharding import PartitionSpec as P

HEADS = 8
HEAD = 64
BLOCK = 128
LOCD = 3
EXPD = 4
VIRT = 16
BLK_DEV = 12
D = 512
NB = 1536
NDEV = 128
PAD = 16
CHUNK = 4
CHUNKS = BLK_DEV // CHUNK
SPAN = CHUNK + 4
NEAR = LOCD * BLOCK
LISTED = (LOCD + EXPD) * BLOCK
KEYS = LISTED + VIRT
KEYS_PAD = 1024
AXES = ("group", "dev")
BF = jnp.bfloat16
F32 = jnp.float32
VMEM_LIMIT = 58 * 1024 * 1024
NT = (((1,), (1,)), ((), ()))


def dot(a, b, dims=None):
    if dims is None:
        return jnp.dot(a, b, preferred_element_type=F32)
    return lax.dot_general(a, b, dims, preferred_element_type=F32)


def params(limit=VMEM_LIMIT):
    return pltpu.CompilerParams(vmem_limit_bytes=limit)


def cost(flops, nbytes):
    return pl.CostEstimate(flops=flops, bytes_accessed=nbytes, transcendentals=0)


def swap_matrix():
    row = lax.broadcasted_iota(jnp.int32, (256, 256), 0)
    col = lax.broadcasted_iota(jnp.int32, (256, 256), 1)
    return jnp.where(col == (row % 16) * 16 + row // 16, 1.0, 0.0).astype(BF)


def stripe_kernel(x_ref, out_ref):
    swap = swap_matrix()[:, : BLK_DEV * 16]
    for g in range(BLOCK // 16):
        rows = x_ref[:, 16 * g : 16 * g + 16, :].reshape(BLK_DEV * 16, D)
        out_ref[16 * g : 16 * g + 16] = dot(swap, rows).astype(BF).reshape(16, PAD, D)


def stripe(x):
    return pl.pallas_call(
        stripe_kernel,
        out_shape=jax.ShapeDtypeStruct((BLOCK, PAD, D), BF),
        compiler_params=params(),
        name="stripe",
    )(x)


def project_kernel(x_ref, w_ref, wt_ref, kv_ref, kvt_ref):
    x = x_ref[...].reshape(4 * BLOCK, D)
    kv_ref[...] = dot(x, w_ref[...]).astype(BF).reshape(4, BLOCK, 2 * D)
    for i in range(4):
        kvt_ref[i] = dot(wt_ref[...], x_ref[i], NT).astype(BF)


def project(x_ext, w_kv, w_kvt):
    n = x_ext.shape[0]
    return pl.pallas_call(
        project_kernel,
        grid=(n // 4,),
        in_specs=[
            pl.BlockSpec((4, BLOCK, D), lambda i: (i, 0, 0)),
            pl.BlockSpec((D, 2 * D), lambda i: (0, 0)),
            pl.BlockSpec((2 * D, D), lambda i: (0, 0)),
        ],
        out_specs=[
            pl.BlockSpec((4, BLOCK, 2 * D), lambda i: (i, 0, 0)),
            pl.BlockSpec((4, 2 * D, BLOCK), lambda i: (i, 0, 0)),
        ],
        out_shape=[
            jax.ShapeDtypeStruct((n, BLOCK, 2 * D), BF),
            jax.ShapeDtypeStruct((n, 2 * D, BLOCK), BF),
        ],
        compiler_params=params(),
        cost_estimate=cost(9_000_000_000, 12_000_000),
        name="project",
    )(x_ext, w_kv, w_kvt)


def reorder_kernel(home_ref, stripes_ref, out_ref):
    rows = out_ref.shape[0]
    at = lax.broadcasted_iota(jnp.int32, (rows, NDEV * PAD), 1)
    pick = jnp.where(home_ref[...] == at, 1.0, 0.0).astype(BF)
    out_ref[...] = dot(pick, stripes_ref[...]).astype(BF)


def reorder(home, stripes):
    step = NB // 2
    return pl.pallas_call(
        reorder_kernel,
        grid=(2,),
        in_specs=[
            pl.BlockSpec((step, 1), lambda i: (i, 0)),
            pl.BlockSpec((NDEV * PAD, D), lambda i: (0, 0)),
        ],
        out_specs=pl.BlockSpec((step, D), lambda i: (i, 0)),
        out_shape=jax.ShapeDtypeStruct((NB, D), BF),
        compiler_params=params(),
        cost_estimate=cost(3_200_000_000, 5_000_000),
        name="reorder",
    )(home, stripes)


def pick_kernel(ids_ref, table_ref, out_ref):
    rows = out_ref.shape[0]
    at = lax.broadcasted_iota(jnp.int32, (rows, NB), 1)
    pick = jnp.where(ids_ref[...] == at, 1.0, 0.0).astype(BF)
    out_ref[...] = dot(pick, table_ref[...]).astype(BF)


def pick_rows(ids, table):
    n = ids.shape[0]
    step = n // 2
    return pl.pallas_call(
        pick_kernel,
        grid=(2,),
        in_specs=[
            pl.BlockSpec((step, 1), lambda i: (i, 0)),
            pl.BlockSpec((NB, D), lambda i: (0, 0)),
        ],
        out_specs=pl.BlockSpec((step, D), lambda i: (i, 0)),
        out_shape=jax.ShapeDtypeStruct((n, D), BF),
        compiler_params=params(),
        cost_estimate=cost(4_000_000_000, 5_000_000),
        name="pick_rows",
    )(ids, table)


def add_kernel(ids_ref, rows_ref, acc_ref, out_ref):
    n = rows_ref.shape[0]
    step = 512
    for i in range(NB // step):
        at = lax.broadcasted_iota(jnp.int32, (step, n), 0) + i * step
        pick = jnp.where(ids_ref[...] == at, 1.0, 0.0).astype(BF)
        part = slice(i * step, (i + 1) * step)
        out_ref[part] = acc_ref[part] + dot(pick, rows_ref[...])


def add_rows(ids, rows, acc):
    return pl.pallas_call(
        add_kernel,
        out_shape=jax.ShapeDtypeStruct((NB, D), F32),
        compiler_params=params(),
        cost_estimate=cost(4_000_000_000, 8_000_000),
        name="add_rows",
    )(ids, rows, acc)


def last_add_kernel(ids_ref, rows_ref, acc_ref, home_ref, out_ref, total):
    n = rows_ref.shape[0]
    step = 512
    for i in range(NB // step):
        at = lax.broadcasted_iota(jnp.int32, (step, n), 0) + i * step
        pick = jnp.where(ids_ref[...] == at, 1.0, 0.0).astype(BF)
        part = slice(i * step, (i + 1) * step)
        total[part] = (acc_ref[part] + dot(pick, rows_ref[...])).astype(BF)
    for i in range(NDEV * PAD // step):
        at = lax.broadcasted_iota(jnp.int32, (step, NB), 0) + i * step
        pick = jnp.where(home_ref[...] == at, 1.0, 0.0).astype(BF)
        out_ref[i * step : (i + 1) * step] = dot(pick, total[...]).astype(BF)


def last_add_rows(ids, rows, acc, home):
    return pl.pallas_call(
        last_add_kernel,
        out_shape=jax.ShapeDtypeStruct((NDEV * PAD, D), BF),
        scratch_shapes=[pltpu.VMEM((NB, D), BF)],
        compiler_params=params(),
        cost_estimate=cost(8_000_000_000, 8_000_000),
        name="last_add_rows",
    )(ids, rows, acc, home)


def finish_kernel(base_ref, far_ref, out_ref):
    swap = swap_matrix()[: BLK_DEV * 16]
    for g in range(BLOCK // 16):
        part = slice(16 * g, 16 * g + 16)
        rows = dot(swap, far_ref[part].reshape(256, D)).reshape(BLK_DEV, 16, D)
        out_ref[:, part] = (base_ref[:, part] + rows).astype(BF)


def finish(base, far):
    return pl.pallas_call(
        finish_kernel,
        out_shape=jax.ShapeDtypeStruct((BLK_DEV, BLOCK, D), BF),
        compiler_params=params(),
        name="finish",
    )(base, far)


def attention_kernel(
    rel_ref,
    live_ref,
    x_ref,
    grad_ref,
    kvx_ref,
    kvtx_ref,
    far_ref,
    vkv_ref,
    vkvt_ref,
    wqt_ref,
    wkv_ref,
    wkvt_ref,
    wo_ref,
    mixed_ref,
    dq_ref,
    near_ref,
    back_ref,
    kv,
    kvt,
    xs,
    ys,
    far_grads,
    near_grads,
    pairs,
    sides,
    bias,
    att,
    dqt,
):
    b = pl.program_id(0)

    @pl.when(b == 0)
    def _():
        near_ref[...] = jnp.zeros_like(near_ref)
        pairs[:, KEYS:, :] = jnp.zeros((2, KEYS_PAD - KEYS, 2 * BLOCK), BF)
        sides[...] = jnp.zeros_like(sides)
        kv[LISTED:KEYS, :] = vkv_ref[...]
        kvt[:, LISTED:KEYS_PAD] = vkvt_ref[...]
        bias[LISTED:KEYS, :] = jnp.zeros((VIRT, BLOCK), F32)
        swap = swap_matrix()
        for g in range(BLOCK // 16):
            part = slice(16 * g, 16 * g + 16)
            rows = dot(swap, far_ref[part].reshape(256, D)).astype(BF)
            xs[:, part, :] = rows.reshape(PAD, 16, D)

    far_x = xs[pl.ds(b * EXPD, EXPD)].reshape(EXPD * BLOCK, D)
    kv[NEAR:LISTED, :] = dot(far_x, wkv_ref[...]).astype(BF)
    kvt[:, NEAR:LISTED] = dot(wkvt_ref[...], far_x, NT).astype(BF)
    for s in range(LOCD):
        part = slice(s * BLOCK, (s + 1) * BLOCK)
        at = rel_ref[b, s]
        kv[part, :] = kvx_ref[at]
        kvt[:, part] = kvtx_ref[at]
    key = lax.broadcasted_iota(jnp.int32, (BLOCK, BLOCK), 0)
    for s in range(LOCD + EXPD):
        part = slice(s * BLOCK, (s + 1) * BLOCK)
        bias[part, :] = jnp.where(key < live_ref[b, s], 0.0, -1e30)
    qt = (dot(wqt_ref[...], x_ref[0], NT).astype(BF) * HEAD**-0.5).astype(BF)
    dat = dot(wo_ref[...], grad_ref[0], NT).astype(BF)
    for h in range(HEADS):
        sides[h, :HEAD, :BLOCK] = qt[h * HEAD : (h + 1) * HEAD]
        sides[h, HEAD:, BLOCK:] = dat[h * HEAD : (h + 1) * HEAD]

    for h in range(HEADS):
        cols = slice(h * 2 * HEAD, (h + 1) * 2 * HEAD)
        rows = slice(h * HEAD, (h + 1) * HEAD)
        side = sides[h]
        pair = pairs.at[h % 2]
        both = dot(kv[:KEYS, cols], side)
        scores = both[:, :BLOCK] + bias[...]
        top = jnp.max(scores, axis=0, keepdims=True)
        weights = jnp.exp(scores - top)
        probs = weights * (1.0 / jnp.sum(weights, axis=0, keepdims=True))
        d_probs = both[:, BLOCK:]
        delta = jnp.sum(probs * d_probs, axis=0, keepdims=True)
        pair[:KEYS, :BLOCK] = (probs * (d_probs - delta)).astype(BF)
        pair[:KEYS, BLOCK:] = probs.astype(BF)
        mixed_in = dot(kvt[cols, :], pair[...])
        dqt[rows, :] = mixed_in[:HEAD, :BLOCK]
        att[rows, :] = mixed_in[HEAD:, BLOCK:]
        key_grads = dot(pair[:LISTED, :], side, NT)
        near_grads[:, cols] = key_grads[:NEAR]
        far_grads[:, cols] = key_grads[NEAR:].astype(BF)

    for s in range(LOCD):
        at = rel_ref[b, s]
        near_ref[at] += near_grads[s * BLOCK : (s + 1) * BLOCK, :]
    mixed_ref[0] = dot(att[...].T.astype(BF), wo_ref[...]).astype(BF)
    dq_ref[0] = (dqt[...] * HEAD**-0.5).T.astype(BF)
    far_term = dot(far_grads[...], wkvt_ref[...]).astype(BF)
    ys[pl.ds(b * EXPD, EXPD)] = far_term.reshape(EXPD, BLOCK, D)

    @pl.when(b == CHUNK - 1)
    def _():
        swap = swap_matrix()
        for g in range(BLOCK // 16):
            part = slice(16 * g, 16 * g + 16)
            rows = dot(swap, ys[:, part, :].reshape(256, D)).astype(BF)
            back_ref[part] = rows.reshape(16, PAD, D)


def attention(c, rel, live, x, grads, kvx, kvtx, far, vkv, vkvt, wqt, wkv, wkvt, wo):
    whole = lambda *shape: pl.BlockSpec(shape, lambda b: (0,) * len(shape))
    rows = pl.BlockSpec((1, BLOCK, D), lambda b: (CHUNK * c + b, 0, 0))
    out_rows = pl.BlockSpec((1, BLOCK, D), lambda b: (b, 0, 0))
    smem = pl.BlockSpec(memory_space=pltpu.SMEM)
    return pl.pallas_call(
        attention_kernel,
        grid=(CHUNK,),
        in_specs=[
            smem,
            smem,
            rows,
            rows,
            whole(SPAN, BLOCK, 2 * D),
            whole(SPAN, 2 * D, BLOCK),
            whole(BLOCK, PAD, D),
            whole(VIRT, 2 * D),
            whole(2 * D, BLOCK),
            whole(D, D),
            whole(D, 2 * D),
            whole(2 * D, D),
            whole(D, D),
        ],
        out_specs=[
            out_rows,
            out_rows,
            whole(SPAN, BLOCK, 2 * D),
            whole(BLOCK, PAD, D),
        ],
        out_shape=[
            jax.ShapeDtypeStruct((CHUNK, BLOCK, D), BF),
            jax.ShapeDtypeStruct((CHUNK, BLOCK, D), BF),
            jax.ShapeDtypeStruct((SPAN, BLOCK, 2 * D), F32),
            jax.ShapeDtypeStruct((BLOCK, PAD, D), BF),
        ],
        scratch_shapes=[
            pltpu.VMEM((KEYS, 2 * D), BF),
            pltpu.VMEM((2 * D, KEYS_PAD), BF),
            pltpu.VMEM((PAD, BLOCK, D), BF),
            pltpu.VMEM((PAD, BLOCK, D), BF),
            pltpu.VMEM((EXPD * BLOCK, 2 * D), BF),
            pltpu.VMEM((NEAR, 2 * D), F32),
            pltpu.VMEM((2, KEYS_PAD, 2 * BLOCK), BF),
            pltpu.VMEM((HEADS, BLOCK, 2 * BLOCK), BF),
            pltpu.VMEM((KEYS, BLOCK), F32),
            pltpu.VMEM((D, BLOCK), F32),
            pltpu.VMEM((D, BLOCK), F32),
        ],
        compiler_params=params(),
        cost_estimate=cost(34_000_000_000, 16_000_000),
        name="attention",
    )(rel, live, x, grads, kvx, kvtx, far, vkv, vkvt, wqt, wkv, wkvt, wo)


def exchange(rows):
    return lax.all_to_all(rows, AXES, split_axis=0, concat_axis=0, tiled=True)


def beside(low, high):
    up = [(i, i + 1) for i in range(NDEV - 1)]
    down = [(j, i) for i, j in up]
    return lax.ppermute(high, AXES, up), lax.ppermute(low, AXES, down)


def on_device(
    node_features,
    virtual_features,
    w_qkv,
    output_weight,
    block_home,
    local_blocks,
    expander_blocks,
    key_live,
    out_grad,
):
    me = lax.axis_index(AXES)
    x = node_features.reshape(BLK_DEV, BLOCK, D)
    grads = out_grad.reshape(BLK_DEV, BLOCK, D)
    stripes = exchange(stripe(x)).reshape(NDEV * PAD, D)

    w_kv = w_qkv[:, D:].reshape(D, 2, HEADS, HEAD).transpose(0, 2, 1, 3).reshape(D, 2 * D)
    w_kvt = w_kv.T
    w_qt = w_qkv[:, :D].T
    vkv = dot(virtual_features, w_kv).astype(BF)
    vkvt = jnp.pad(vkv.T, ((0, 0), (0, BLOCK - VIRT)))

    before, after = beside(x[:2], x[BLK_DEV - 2 :])
    x_ext = jnp.concatenate([before, x, after], axis=0)
    kvx, kvtx = project(x_ext, w_kv, w_kvt)

    graph = jnp.arange(NB, dtype=jnp.int32)
    near_at = jnp.sum(
        jnp.where(local_blocks[:, :, None] == graph, block_home, 0), axis=-1, dtype=jnp.int32
    )
    shift = jnp.arange(BLK_DEV, dtype=jnp.int32)[:, None] // CHUNK * CHUNK
    rel = near_at - (me * BLK_DEV - 2) - shift
    home = block_home // BLK_DEV * PAD + block_home % BLK_DEV
    asked = expander_blocks.reshape(NDEV, CHUNKS, PAD)
    ids = [asked[:, c].reshape(NDEV * PAD) for c in range(CHUNKS)]

    table = reorder(home[:, None], stripes)
    incoming = [
        exchange(pick_rows(ids[c][:, None], table).reshape(NDEV, PAD, D)) for c in range(CHUNKS)
    ]
    mixed, d_query, near, back = [], [], [], []
    for c in range(CHUNKS):
        first = CHUNK * c
        m, dq, na, fb = attention(
            c,
            rel[first : first + CHUNK],
            key_live[first : first + CHUNK],
            x,
            grads,
            kvx[first : first + SPAN],
            kvtx[first : first + SPAN],
            incoming[c],
            vkv,
            vkvt,
            w_qt,
            w_kv,
            w_kvt,
            output_weight,
        )
        mixed.append(m)
        d_query.append(dq)
        near.append(na)
        back.append(exchange(fb).reshape(NDEV * PAD, D))

    low, high = beside(near[0][:2].astype(BF), near[-1][SPAN - 2 :].astype(BF))
    sums = []
    for c in range(CHUNKS):
        total = near[c][2 : 2 + CHUNK]
        prior = low.astype(F32) if c == 0 else near[c - 1][SPAN - 2 :]
        later = high.astype(F32) if c == CHUNKS - 1 else near[c + 1][:2]
        sums.append(total + jnp.concatenate([prior, later], axis=0))
    near_sum = jnp.concatenate(sums, axis=0).astype(BF).reshape(BLK_DEV * BLOCK, 2 * D)
    d_q = jnp.concatenate(d_query, axis=0).reshape(BLK_DEV * BLOCK, D)
    base = dot(d_q, w_qt) + dot(near_sum, w_kvt)

    acc = jnp.zeros((NB, D), F32)
    for c in range(CHUNKS - 1):
        acc = add_rows(ids[c][None, :], back[c], acc)
    far_sum = last_add_rows(ids[-1][None, :], back[-1], acc, home[None, :])
    far = exchange(far_sum.reshape(NDEV, PAD, D))
    node_grad = finish(base.reshape(BLK_DEV, BLOCK, D), far)
    mixed = jnp.concatenate(mixed, axis=0).reshape(BLK_DEV * BLOCK, D)
    return mixed, node_grad.reshape(BLK_DEV * BLOCK, D)


def solution(mesh):
    rows = P(AXES, None)
    return jax.shard_map(
        on_device,
        mesh=mesh,
        in_specs=(rows, P(), P(), P(), P(), rows, P(), rows, rows),
        out_specs=(rows, rows),
        check_vma=False,
    )
```

```python
import jax
import jax.numpy as jnp
from jax import lax
from jax.experimental import pallas as pl
from jax.experimental.pallas import tpu as pltpu
from jax.sharding import PartitionSpec as P

HEADS = 8
HEAD = 64
BLOCK = 128
LOCD = 3
EXPD = 4
VIRT = 16
BLK_DEV = 12
D = 512
NB = 1536
NDEV = 128
PAD = 16
PARTS = ((0, 4), (4, 8))
NEAR = LOCD * BLOCK
LISTED = (LOCD + EXPD) * BLOCK
KEYS = LISTED + VIRT
KEYS_PAD = 1024
AXES = ("group", "dev")
BF = jnp.bfloat16
F32 = jnp.float32
VMEM_LIMIT = 58 * 1024 * 1024
NT = (((1,), (1,)), ((), ()))


def dot(a, b, dims=None):
    if dims is None:
        return jnp.dot(a, b, preferred_element_type=F32)
    return lax.dot_general(a, b, dims, preferred_element_type=F32)


def params(limit=VMEM_LIMIT):
    return pltpu.CompilerParams(vmem_limit_bytes=limit)


def cost(flops, nbytes):
    return pl.CostEstimate(flops=flops, bytes_accessed=nbytes, transcendentals=0)


def swap_matrix():
    row = lax.broadcasted_iota(jnp.int32, (256, 256), 0)
    col = lax.broadcasted_iota(jnp.int32, (256, 256), 1)
    return jnp.where(col == (row % 16) * 16 + row // 16, 1.0, 0.0).astype(BF)


def stripe_kernel(x_ref, out_ref):
    swap = swap_matrix()[:, : BLK_DEV * 16]
    for g in range(BLOCK // 16):
        rows = x_ref[:, 16 * g : 16 * g + 16, :].reshape(BLK_DEV * 16, D)
        out_ref[16 * g : 16 * g + 16] = dot(swap, rows).astype(BF).reshape(16, PAD, D)


def stripe(x):
    return pl.pallas_call(
        stripe_kernel,
        out_shape=jax.ShapeDtypeStruct((BLOCK, PAD, D), BF),
        compiler_params=params(),
        name="stripe",
    )(x)


def project_kernel(x_ref, w_ref, wt_ref, kv_ref, kvt_ref):
    x = x_ref[...].reshape(4 * BLOCK, D)
    kv_ref[...] = dot(x, w_ref[...]).astype(BF).reshape(4, BLOCK, 2 * D)
    for i in range(4):
        kvt_ref[i] = dot(wt_ref[...], x_ref[i], NT).astype(BF)


def project(x_ext, w_kv, w_kvt):
    n = x_ext.shape[0]
    return pl.pallas_call(
        project_kernel,
        grid=(n // 4,),
        in_specs=[
            pl.BlockSpec((4, BLOCK, D), lambda i: (i, 0, 0)),
            pl.BlockSpec((D, 2 * D), lambda i: (0, 0)),
            pl.BlockSpec((2 * D, D), lambda i: (0, 0)),
        ],
        out_specs=[
            pl.BlockSpec((4, BLOCK, 2 * D), lambda i: (i, 0, 0)),
            pl.BlockSpec((4, 2 * D, BLOCK), lambda i: (i, 0, 0)),
        ],
        out_shape=[
            jax.ShapeDtypeStruct((n, BLOCK, 2 * D), BF),
            jax.ShapeDtypeStruct((n, 2 * D, BLOCK), BF),
        ],
        compiler_params=params(),
        cost_estimate=cost(9_000_000_000, 12_000_000),
        name="project",
    )(x_ext, w_kv, w_kvt)


def pick_kernel(at_ref, stripes_ref, out_ref):
    at = lax.broadcasted_iota(jnp.int32, (out_ref.shape[0], NDEV * PAD), 1)
    pick = jnp.where(at_ref[...] == at, 1.0, 0.0).astype(BF)
    out_ref[...] = dot(pick, stripes_ref[...]).astype(BF)


def pick_rows(at, stripes):
    n = at.shape[0]
    step = 512
    return pl.pallas_call(
        pick_kernel,
        grid=(n // step,),
        in_specs=[
            pl.BlockSpec((step, 1), lambda i: (i, 0)),
            pl.BlockSpec((NDEV * PAD, D), lambda i: (0, 0)),
        ],
        out_specs=pl.BlockSpec((step, D), lambda i: (i, 0)),
        out_shape=jax.ShapeDtypeStruct((n, D), BF),
        compiler_params=params(),
        cost_estimate=cost(2 * n * NDEV * PAD * D, 6_000_000),
        name="pick_rows",
    )(at, stripes)


def add_kernel(at_ref, rows_ref, *refs):
    out_ref = refs[-1]
    step, n = out_ref.shape[0], rows_ref.shape[0]
    at = lax.broadcasted_iota(jnp.int32, (step, n), 0) + pl.program_id(0) * step
    pick = jnp.where(at_ref[...] == at, 1.0, 0.0).astype(BF)
    total = dot(pick, rows_ref[...])
    if len(refs) > 1:
        total += refs[0][...]
    out_ref[...] = total.astype(out_ref.dtype)


def add_rows(at, rows, acc, dtype):
    n = rows.shape[0]
    step = 512
    part = pl.BlockSpec((step, D), lambda i: (i, 0))
    return pl.pallas_call(
        add_kernel,
        grid=(NDEV * PAD // step,),
        in_specs=[
            pl.BlockSpec((1, n), lambda i: (0, 0)),
            pl.BlockSpec((n, D), lambda i: (0, 0)),
        ]
        + [part] * len(acc),
        out_specs=part,
        out_shape=jax.ShapeDtypeStruct((NDEV * PAD, D), dtype),
        compiler_params=params(),
        cost_estimate=cost(2 * n * NDEV * PAD * D, 8_000_000),
        name="add_rows",
    )(at, rows, *acc)


def finish_kernel(base_ref, far_ref, out_ref):
    swap = swap_matrix()[: BLK_DEV * 16]
    for g in range(BLOCK // 16):
        part = slice(16 * g, 16 * g + 16)
        rows = dot(swap, far_ref[part].reshape(256, D)).reshape(BLK_DEV, 16, D)
        out_ref[:, part] = (base_ref[:, part] + rows).astype(BF)


def finish(base, far):
    return pl.pallas_call(
        finish_kernel,
        out_shape=jax.ShapeDtypeStruct((BLK_DEV, BLOCK, D), BF),
        compiler_params=params(),
        name="finish",
    )(base, far)


def attention_kernel(
    rel_ref,
    live_ref,
    x_ref,
    grad_ref,
    kvx_ref,
    kvtx_ref,
    far_ref,
    vkv_ref,
    vkvt_ref,
    wqt_ref,
    wkv_ref,
    wkvt_ref,
    wo_ref,
    mixed_ref,
    dq_ref,
    near_ref,
    back_ref,
    kv,
    kvt,
    far_rows,
    far_grads,
    near_grads,
    pairs,
    sides,
    bias,
    att,
    dqt,
    both,
):
    b = pl.program_id(0)

    @pl.when(b == 0)
    def _():
        near_ref[...] = jnp.zeros_like(near_ref)
        pairs[:, KEYS:, :] = jnp.zeros((2, KEYS_PAD - KEYS, 2 * BLOCK), BF)
        sides[...] = jnp.zeros_like(sides)
        kv[LISTED:KEYS, :] = vkv_ref[...]
        kvt[:, LISTED:KEYS_PAD] = vkvt_ref[...]
        bias[LISTED:KEYS, :] = jnp.zeros((VIRT, BLOCK), BF)
        lane = lax.broadcasted_iota(jnp.int32, (BLOCK, 2 * BLOCK), 1)
        row = lax.broadcasted_iota(jnp.int32, (BLOCK, 2 * BLOCK), 0)
        ones = jnp.where((row == 0) & (lane < BLOCK), 1.0, 0.0).astype(BF)
        for h in range(HEADS):
            sides[h, BLOCK:, :] = ones
        swap = swap_matrix()
        for u in range(0, far_ref.shape[1], 16):
            for g in range(0, BLOCK, 16):
                rows = dot(swap, far_ref[g : g + 16, u : u + 16, :].reshape(256, D)).astype(BF)
                far_rows[u : u + 16, g : g + 16, :] = rows.reshape(16, 16, D)

    far_x = far_rows[pl.ds(b * EXPD, EXPD)].reshape(EXPD * BLOCK, D)
    kv[NEAR:LISTED, :] = dot(far_x, wkv_ref[...]).astype(BF)
    kvt[:, NEAR:LISTED] = dot(wkvt_ref[...], far_x, NT).astype(BF)
    for s in range(LOCD):
        part = slice(s * BLOCK, (s + 1) * BLOCK)
        at = rel_ref[b, s]
        kv[part, :] = kvx_ref[at]
        kvt[:, part] = kvtx_ref[at]
    key = lax.broadcasted_iota(jnp.int32, (BLOCK, BLOCK), 0)
    lane = lax.broadcasted_iota(jnp.int32, (BLOCK, BLOCK), 1)
    for s in range(LOCD + EXPD):
        part = slice(s * BLOCK, (s + 1) * BLOCK)
        bias[part, :] = jnp.where((key < live_ref[b, s]) | (lane > 0), 0.0, -1e30).astype(BF)
    qt = (dot(wqt_ref[...], x_ref[0], NT).astype(BF) * HEAD**-0.5).astype(BF)
    dat = dot(wo_ref[...], grad_ref[0], NT).astype(BF)
    for h in range(HEADS):
        sides[h, :HEAD, :BLOCK] = qt[h * HEAD : (h + 1) * HEAD]
        sides[h, HEAD:BLOCK, BLOCK:] = dat[h * HEAD : (h + 1) * HEAD]

    def head_cols(h):
        return slice(h * 2 * HEAD, (h + 1) * 2 * HEAD)

    def score(h):
        keys = jnp.concatenate([kv[:, head_cols(h)], bias[...]], axis=1)
        both[h % 2] = dot(keys, sides[h])

    def soften(h):
        now = both.at[h % 2]
        pair = pairs.at[h % 2]
        step = 48
        folded = (step // 8, 8, BLOCK)
        parts = [slice(r, r + step) for r in range(0, KEYS, step)]
        top = jnp.full((8, BLOCK), -jnp.inf, F32)
        for part in parts:
            top = jnp.maximum(top, jnp.max(now[part, :BLOCK].reshape(folded), axis=0))
        top = jnp.max(top, axis=0, keepdims=True)
        total = jnp.zeros((8, BLOCK), F32)
        drift = jnp.zeros((8, BLOCK), F32)
        for part in parts:
            weights = jnp.exp(now[part, :BLOCK] - top)
            now[part, :BLOCK] = weights
            total += jnp.sum(weights.reshape(folded), axis=0)
            drift += jnp.sum((weights * now[part, BLOCK:]).reshape(folded), axis=0)
        inverse = 1.0 / jnp.sum(total, axis=0, keepdims=True)
        delta = jnp.sum(drift, axis=0, keepdims=True) * inverse
        for part in parts:
            probs = now[part, :BLOCK] * inverse
            pair[part, :BLOCK] = (probs * (now[part, BLOCK:] - delta)).astype(BF)
            pair[part, BLOCK:] = probs.astype(BF)

    def gather_up(h):
        cols = head_cols(h)
        rows = slice(h * HEAD, (h + 1) * HEAD)
        pair = pairs.at[h % 2]
        mixed_in = dot(kvt[cols, :], pair[...])
        dqt[rows, :] = mixed_in[:HEAD, :BLOCK]
        att[rows, :] = mixed_in[HEAD:, BLOCK:]
        key_grads = dot(pair[:LISTED, :], sides[h, :BLOCK, :], NT)
        near_grads[:, cols] = key_grads[:NEAR]
        far_grads[:, cols] = key_grads[NEAR:].astype(BF)

    score(0)
    for h in range(HEADS):
        if h + 1 < HEADS:
            score(h + 1)
        soften(h)
        if h > 0:
            gather_up(h - 1)
    gather_up(HEADS - 1)

    for s in range(LOCD):
        at = rel_ref[b, s]
        near_ref[at] += near_grads[s * BLOCK : (s + 1) * BLOCK, :]
    mixed_ref[0] = dot(att[...].T.astype(BF), wo_ref[...]).astype(BF)
    dq_ref[0] = (dqt[...] * HEAD**-0.5).T.astype(BF)
    far_term = dot(far_grads[...], wkvt_ref[...]).astype(BF)
    far_rows[pl.ds(b * EXPD, EXPD)] = far_term.reshape(EXPD, BLOCK, D)

    @pl.when(b == pl.num_programs(0) - 1)
    def _():
        swap = swap_matrix()
        for u in range(0, far_ref.shape[1], 16):
            for g in range(0, BLOCK, 16):
                rows = far_rows[u : u + 16, g : g + 16, :].reshape(256, D)
                back_ref[g : g + 16, u : u + 16, :] = dot(swap, rows).astype(BF).reshape(16, 16, D)


def attention(first, rel, live, x, grads, kvx, kvtx, far, vkv, vkvt, wqt, wkv, wkvt, wo):
    count = rel.shape[0]
    span, listed = count + 4, count * EXPD

    def whole(*shape):
        return pl.BlockSpec(shape, lambda b: (0,) * len(shape), pipeline_mode=pl.Buffered(1))

    def kept(*shape):
        return pl.BlockSpec(shape, lambda b: (0,) * len(shape))

    rows = pl.BlockSpec((1, BLOCK, D), lambda b: (first + b, 0, 0))
    out_rows = pl.BlockSpec((1, BLOCK, D), lambda b: (b, 0, 0))
    smem = pl.BlockSpec(memory_space=pltpu.SMEM)
    return pl.pallas_call(
        attention_kernel,
        grid=(count,),
        in_specs=[
            smem,
            smem,
            rows,
            rows,
            whole(span, BLOCK, 2 * D),
            whole(span, 2 * D, BLOCK),
            whole(BLOCK, listed, D),
            whole(VIRT, 2 * D),
            whole(2 * D, BLOCK),
            whole(D, D),
            whole(D, 2 * D),
            whole(2 * D, D),
            whole(D, D),
        ],
        out_specs=[
            out_rows,
            out_rows,
            kept(span, BLOCK, 2 * D),
            kept(BLOCK, listed, D),
        ],
        out_shape=[
            jax.ShapeDtypeStruct((count, BLOCK, D), BF),
            jax.ShapeDtypeStruct((count, BLOCK, D), BF),
            jax.ShapeDtypeStruct((span, BLOCK, 2 * D), F32),
            jax.ShapeDtypeStruct((BLOCK, listed, D), BF),
        ],
        scratch_shapes=[
            pltpu.VMEM((KEYS, 2 * D), BF),
            pltpu.VMEM((2 * D, KEYS_PAD), BF),
            pltpu.VMEM((listed, BLOCK, D), BF),
            pltpu.VMEM((EXPD * BLOCK, 2 * D), BF),
            pltpu.VMEM((NEAR, 2 * D), F32),
            pltpu.VMEM((2, KEYS_PAD, 2 * BLOCK), BF),
            pltpu.VMEM((HEADS, 2 * BLOCK, 2 * BLOCK), BF),
            pltpu.VMEM((KEYS, BLOCK), BF),
            pltpu.VMEM((D, BLOCK), F32),
            pltpu.VMEM((D, BLOCK), F32),
            pltpu.VMEM((2, KEYS, 2 * BLOCK), F32),
        ],
        compiler_params=params(),
        cost_estimate=cost(count * 9_000_000_000, 20_000_000),
        name="attention",
    )(rel, live, x, grads, kvx, kvtx, far, vkv, vkvt, wqt, wkv, wkvt, wo)


def exchange(rows):
    return lax.all_to_all(rows, AXES, split_axis=0, concat_axis=0, tiled=True)


def beside(low, high):
    up = [(i, i + 1) for i in range(NDEV - 1)]
    down = [(j, i) for i, j in up]
    return lax.ppermute(high, AXES, up), lax.ppermute(low, AXES, down)


def on_device(
    node_features,
    virtual_features,
    w_qkv,
    output_weight,
    block_home,
    local_blocks,
    expander_blocks,
    key_live,
    out_grad,
):
    me = lax.axis_index(AXES)
    x = node_features.reshape(BLK_DEV, BLOCK, D)
    grads = out_grad.reshape(BLK_DEV, BLOCK, D)
    stripes = exchange(stripe(x)).reshape(NDEV * PAD, D)
    before, after = beside(x[:2], x[BLK_DEV - 2 :])

    w_kv = w_qkv[:, D:].reshape(D, 2, HEADS, HEAD).transpose(0, 2, 1, 3).reshape(D, 2 * D)
    w_kvt = w_kv.T
    w_qt = w_qkv[:, :D].T
    vkv = dot(virtual_features, w_kv).astype(BF)
    vkvt = jnp.pad(vkv.T, ((0, 0), (0, BLOCK - VIRT)))
    x_ext = jnp.concatenate([before, x, after], axis=0)

    graph = jnp.arange(NB, dtype=jnp.int32)

    def stored_at(ids, home):
        same = ids[..., None] == graph
        return jnp.sum(jnp.where(same, home, 0), axis=-1, dtype=jnp.int32)

    near_at = stored_at(local_blocks, block_home)
    rel = near_at - (me * BLK_DEV - 2)
    home = block_home // BLK_DEV * PAD + block_home % BLK_DEV
    far_at = stored_at(expander_blocks.reshape(NDEV, BLK_DEV * EXPD), home)
    at = [far_at[:, EXPD * f : EXPD * (f + n)].reshape(-1) for f, n in PARTS]
    tall = [a[:, None] for a in at]
    stripes, x_ext, w_kv, w_kvt, w_qt, vkv, vkvt, rel, tall, at = lax.optimization_barrier(
        (stripes, x_ext, w_kv, w_kvt, w_qt, vkv, vkvt, rel, tall, at)
    )

    rows = pick_rows(tall[0], stripes)
    incoming = exchange(rows.reshape(NDEV, -1, D))
    later = pick_rows(tall[1], stripes)
    kvx, kvtx = project(x_ext, w_kv, w_kvt)
    near_kv = [(kvx[f : f + n + 4], kvtx[f : f + n + 4]) for f, n in PARTS]
    incoming, later, near_kv = lax.optimization_barrier((incoming, later, near_kv))
    incoming = [incoming, exchange(later.reshape(NDEV, -1, D))]

    mixed, d_query, near, back = [], [], [], []
    for c, (first, count) in enumerate(PARTS):
        m, dq, na, fb = attention(
            first,
            rel[first : first + count] - first,
            key_live[first : first + count],
            x,
            grads,
            *near_kv[c],
            incoming[c],
            vkv,
            vkvt,
            w_qt,
            w_kv,
            w_kvt,
            output_weight,
        )
        mixed.append(m)
        d_query.append(dq)
        near.append(na)
        back.append(exchange(fb).reshape(-1, D))

    low, high = beside(near[0][:2].astype(BF), near[-1][-2:].astype(BF))
    sums = []
    for c, (first, count) in enumerate(PARTS):
        total = near[c][2 : 2 + count]
        prior = low.astype(F32) if c == 0 else near[c - 1][-2:]
        nextp = high.astype(F32) if c == len(PARTS) - 1 else near[c + 1][:2]
        rest = jnp.zeros((count - 4, BLOCK, 2 * D), F32)
        sums.append(total + jnp.concatenate([prior, rest, nextp], axis=0))
    near_sum = jnp.concatenate(sums, axis=0).astype(BF).reshape(BLK_DEV * BLOCK, 2 * D)
    d_q = jnp.concatenate(d_query, axis=0).reshape(BLK_DEV * BLOCK, D)
    base = dot(d_q, w_qt) + dot(near_sum, w_kvt)

    acc = add_rows(at[0][None, :], back[0], (), F32)
    far_sum = add_rows(at[1][None, :], back[1], (acc,), BF)
    far = exchange(far_sum.reshape(NDEV, PAD, D))
    node_grad = finish(base.reshape(BLK_DEV, BLOCK, D), far)
    mixed = jnp.concatenate(mixed, axis=0).reshape(BLK_DEV * BLOCK, D)
    return mixed, node_grad.reshape(BLK_DEV * BLOCK, D)


def solution(mesh):
    rows = P(AXES, None)
    return jax.shard_map(
        on_device,
        mesh=mesh,
        in_specs=(rows, P(), P(), P(), P(), rows, P(), rows, rows),
        out_specs=(rows, rows),
        check_vma=False,
    )
```

```python
import jax
import jax.numpy as jnp
from jax import lax
from jax.experimental import pallas as pl
from jax.experimental.pallas import tpu as pltpu
from jax.sharding import PartitionSpec as P

HEADS = 8
HEAD = 64
BLOCK = 128
LOCD = 3
EXPD = 4
VIRT = 16
BLK_DEV = 12
D = 512
NB = 1536
NDEV = 128
FOLD = 8
WIDE = D + D // 2
HALF = D // 2
SPLIT = 2048
PARTS = ((0, 4), (4, 8))
NEAR = LOCD * BLOCK
LISTED = (LOCD + EXPD) * BLOCK
KEYS = LISTED + VIRT
AXES = ("group", "dev")
BF = jnp.bfloat16
F32 = jnp.float32
VMEM_LIMIT = 58 * 1024 * 1024
NT = (((1,), (1,)), ((), ()))
TN = (((0,), (0,)), ((), ()))


def dot(a, b, dims=None):
    if dims is None:
        return jnp.dot(a, b, preferred_element_type=F32)
    return lax.dot_general(a, b, dims, preferred_element_type=F32)


def params(limit=VMEM_LIMIT):
    return pltpu.CompilerParams(vmem_limit_bytes=limit)


def cost(flops, nbytes):
    return pl.CostEstimate(flops=flops, bytes_accessed=nbytes, transcendentals=0)


def swap_matrix():
    row = lax.broadcasted_iota(jnp.int32, (256, 256), 0)
    col = lax.broadcasted_iota(jnp.int32, (256, 256), 1)
    return jnp.where(col == (row % 16) * 16 + row // 16, 1.0, 0.0).astype(BF)


def fold_matrices(transposed):
    shape = (BLK_DEV * 16, 16 * FOLD) if transposed else (16 * FOLD, BLK_DEV * 16)
    folded = lax.broadcasted_iota(jnp.int32, shape, 1 if transposed else 0)
    plain = lax.broadcasted_iota(jnp.int32, shape, 0 if transposed else 1)
    same = folded // FOLD == plain % 16
    row, block = folded % FOLD, plain // 16
    return [
        jnp.where(same & hit, 1.0, 0.0).astype(BF)
        for hit in (block == row, (block == row + 8) & (row < 4), (block == row + 4) & (row >= 4))
    ]


def stripe_kernel(x_ref, out_ref):
    whole, left, right = fold_matrices(False)
    for g in range(BLOCK // 16):
        rows = x_ref[:, 16 * g : 16 * g + 16, :].reshape(BLK_DEV * 16, D)
        part = slice(16 * FOLD * g, 16 * FOLD * (g + 1))
        out_ref[part, :D] = dot(whole, rows).astype(BF)
        out_ref[part, D:] = (dot(left, rows[:, :HALF]) + dot(right, rows[:, HALF:])).astype(BF)


def stripe(x):
    return pl.pallas_call(
        stripe_kernel,
        out_shape=jax.ShapeDtypeStruct((BLOCK * FOLD, WIDE), BF),
        compiler_params=params(),
        name="stripe",
    )(x)


def project_kernel(x_ref, w_ref, kv_ref):
    kv_ref[...] = dot(x_ref[...].reshape(4 * BLOCK, D), w_ref[...]).astype(BF).reshape(4, BLOCK, 2 * D)


def project(x_ext, w_kv, first, count):
    return pl.pallas_call(
        project_kernel,
        grid=(count // 4,),
        in_specs=[
            pl.BlockSpec((4, BLOCK, D), lambda i: (first // 4 + i, 0, 0)),
            pl.BlockSpec((D, 2 * D), lambda i: (0, 0)),
        ],
        out_specs=pl.BlockSpec((4, BLOCK, 2 * D), lambda i: (i, 0, 0)),
        out_shape=jax.ShapeDtypeStruct((count, BLOCK, 2 * D), BF),
        compiler_params=params(),
        cost_estimate=cost(count * 150_000_000, 12_000_000),
        name="project",
    )(x_ext, w_kv)


def sides_kernel(x_ref, grad_ref, wqt_ref, wo_ref, out_ref):
    out_ref[...] = jnp.zeros_like(out_ref)
    qt = (dot(wqt_ref[...], x_ref[...].reshape(-1, D), NT).astype(BF) * HEAD**-0.5).astype(BF)
    dat = dot(wo_ref[...], grad_ref[...].reshape(-1, D), NT).astype(BF)
    for i in range(x_ref.shape[0]):
        part = slice(i * BLOCK, (i + 1) * BLOCK)
        for h in range(HEADS):
            out_ref[i, h, :HEAD, :BLOCK] = qt[h * HEAD : (h + 1) * HEAD, part]
            out_ref[i, h, HEAD:, BLOCK:] = dat[h * HEAD : (h + 1) * HEAD, part]


def make_sides(x, grads, w_qt, wo):
    step = 4
    rows = pl.BlockSpec((step, BLOCK, D), lambda i: (i, 0, 0))
    weight = pl.BlockSpec((D, D), lambda i: (0, 0))
    return pl.pallas_call(
        sides_kernel,
        grid=(BLK_DEV // step,),
        in_specs=[rows, rows, weight, weight],
        out_specs=pl.BlockSpec((step, HEADS, BLOCK, 2 * BLOCK), lambda i: (i, 0, 0, 0)),
        out_shape=jax.ShapeDtypeStruct((BLK_DEV, HEADS, BLOCK, 2 * BLOCK), BF),
        compiler_params=params(),
        cost_estimate=cost(2_000_000_000, 12_000_000),
        name="make_sides",
    )(x, grads, w_qt, wo)


def picked(codes, at):
    return [
        jnp.where(codes == at + shift, 1.0, 0.0).astype(BF) for shift in (0, SPLIT, SPLIT - 4)
    ]


def pick_kernel(codes_ref, stripes_ref, out_ref):
    at = lax.broadcasted_iota(jnp.int32, (out_ref.shape[0], NDEV * FOLD), 1)
    whole, left, right = picked(codes_ref[...], at)
    rows = dot(whole, stripes_ref[:, :D])
    halves = stripes_ref[:, D:]
    out_ref[:, :HALF] = (rows[:, :HALF] + dot(left, halves)).astype(BF)
    out_ref[:, HALF:] = (rows[:, HALF:] + dot(right, halves)).astype(BF)


def pick_rows(codes, stripes):
    n = codes.shape[0]
    step = 512
    return pl.pallas_call(
        pick_kernel,
        grid=(n // step,),
        in_specs=[
            pl.BlockSpec((step, 1), lambda i: (i, 0)),
            pl.BlockSpec((NDEV * FOLD, WIDE), lambda i: (0, 0)),
        ],
        out_specs=pl.BlockSpec((step, D), lambda i: (i, 0)),
        out_shape=jax.ShapeDtypeStruct((n, D), BF),
        compiler_params=params(),
        cost_estimate=cost(n * 2_100_000, 6_000_000),
        name="pick_rows",
    )(codes, stripes)


def add_kernel(codes_ref, rows_ref, *refs):
    out_ref = refs[-1]
    step, n = out_ref.shape[0], rows_ref.shape[0]
    at = lax.broadcasted_iota(jnp.int32, (step, n), 0) + pl.program_id(0) * step
    whole, left, right = picked(codes_ref[...], at)
    main = dot(whole, rows_ref[...])
    halves = dot(left, rows_ref[:, :HALF]) + dot(right, rows_ref[:, HALF:])
    if len(refs) > 1:
        main += refs[0][:, :D]
        halves += refs[0][:, D:]
    out_ref[:, :D] = main.astype(out_ref.dtype)
    out_ref[:, D:] = halves.astype(out_ref.dtype)


def add_rows(codes, rows, acc, dtype):
    n = rows.shape[0]
    step = 256
    part = pl.BlockSpec((step, WIDE), lambda i: (i, 0))
    return pl.pallas_call(
        add_kernel,
        grid=(NDEV * FOLD // step,),
        in_specs=[
            pl.BlockSpec((1, n), lambda i: (0, 0)),
            pl.BlockSpec((n, D), lambda i: (0, 0)),
        ]
        + [part] * len(acc),
        out_specs=part,
        out_shape=jax.ShapeDtypeStruct((NDEV * FOLD, WIDE), dtype),
        compiler_params=params(),
        cost_estimate=cost(n * 2_100_000, 8_000_000),
        name="add_rows",
    )(codes, rows, *acc)


def finish_kernel(base_ref, far_ref, out_ref):
    whole, left, right = fold_matrices(True)
    for g in range(BLOCK // 16):
        part = slice(16 * g, 16 * g + 16)
        rows = far_ref[16 * FOLD * g : 16 * FOLD * (g + 1)]
        main = dot(whole, rows[:, :D])
        halves = rows[:, D:]
        low = (main[:, :HALF] + dot(left, halves)).reshape(BLK_DEV, 16, HALF)
        high = (main[:, HALF:] + dot(right, halves)).reshape(BLK_DEV, 16, HALF)
        out_ref[:, part, :HALF] = (base_ref[:, part, :HALF] + low).astype(BF)
        out_ref[:, part, HALF:] = (base_ref[:, part, HALF:] + high).astype(BF)


def finish(base, far):
    return pl.pallas_call(
        finish_kernel,
        out_shape=jax.ShapeDtypeStruct((BLK_DEV, BLOCK, D), BF),
        compiler_params=params(),
        name="finish",
    )(base, far)


def head_cols(h):
    return slice(h * 2 * HEAD, (h + 1) * 2 * HEAD)


def far_kernel(
    rel_ref,
    live_ref,
    sides_ref,
    kvx_ref,
    far_ref,
    vkv_ref,
    wkv_ref,
    wkvt_ref,
    back_ref,
    pairs_ref,
    kv_ref,
    far_rows,
    far_grads,
    bias,
    ones,
    both,
):
    b = pl.program_id(0)
    kv = kv_ref.at[0]

    @pl.when(b == 0)
    def _():
        bias[LISTED:KEYS, :] = jnp.zeros((VIRT, BLOCK), BF)
        lane = lax.broadcasted_iota(jnp.int32, (BLOCK, 2 * BLOCK), 1)
        row = lax.broadcasted_iota(jnp.int32, (BLOCK, 2 * BLOCK), 0)
        ones[...] = jnp.where((row == 0) & (lane < BLOCK), 1.0, 0.0).astype(BF)
        swap = swap_matrix()
        for u in range(0, far_ref.shape[1], 16):
            for g in range(0, BLOCK, 16):
                rows = dot(swap, far_ref[g : g + 16, u : u + 16, :].reshape(256, D)).astype(BF)
                far_rows[u : u + 16, g : g + 16, :] = rows.reshape(16, 16, D)

    far_x = far_rows[pl.ds(b * EXPD, EXPD)].reshape(EXPD * BLOCK, D)
    kv[NEAR:LISTED, :] = dot(far_x, wkv_ref[...]).astype(BF)
    kv[LISTED:KEYS, :] = vkv_ref[...]
    for s in range(LOCD):
        kv[s * BLOCK : (s + 1) * BLOCK, :] = kvx_ref[rel_ref[b, s]]
    key = lax.broadcasted_iota(jnp.int32, (BLOCK, BLOCK), 0)
    lane = lax.broadcasted_iota(jnp.int32, (BLOCK, BLOCK), 1)
    for s in range(LOCD + EXPD):
        part = slice(s * BLOCK, (s + 1) * BLOCK)
        closed = (key >= live_ref[b, s]) & (lane == 0)
        bias[part, :] = jnp.where(closed, -1e30, 0.0).astype(BF)

    def products(h):
        if h < HEADS:
            side = jnp.concatenate([sides_ref[0, h], ones[...]], axis=0)
            for part in (slice(0, 464), slice(464, KEYS)):
                keys = jnp.concatenate([kv[part, head_cols(h)], bias[part, :]], axis=1)
                both[h % 2, part, :] = dot(keys, side)
                yield
        g = h - 2
        if g >= 0:
            pair = pairs_ref[0, g, NEAR:LISTED, :]
            far_grads[:, head_cols(g)] = dot(pair, sides_ref[0, g], NT).astype(BF)
            yield

    def soften(h):
        if h < 0 or h >= HEADS:
            return
        now = both.at[h % 2]
        pair = pairs_ref.at[0, h]
        step = 48
        folded = (step // 8, 8, BLOCK)
        parts = [slice(r, r + step) for r in range(0, KEYS, step)]
        top = jnp.full((8, BLOCK), -jnp.inf, F32)
        for part in parts:
            top = jnp.maximum(top, jnp.max(now[part, :BLOCK].reshape(folded), axis=0))
            yield
        top = jnp.max(top, axis=0, keepdims=True)
        total = jnp.zeros((8, BLOCK), F32)
        drift = jnp.zeros((8, BLOCK), F32)
        for part in parts:
            weights = jnp.exp(now[part, :BLOCK] - top)
            now[part, :BLOCK] = weights
            total += jnp.sum(weights.reshape(folded), axis=0)
            drift += jnp.sum((weights * now[part, BLOCK:]).reshape(folded), axis=0)
            yield
        inverse = 1.0 / jnp.sum(total, axis=0, keepdims=True)
        delta = jnp.sum(drift, axis=0, keepdims=True) * inverse
        for part in parts:
            probs = now[part, :BLOCK] * inverse
            pair[part, :BLOCK] = (probs * (now[part, BLOCK:] - delta)).astype(BF)
            pair[part, BLOCK:] = probs.astype(BF)
            yield

    done = object()
    for h in range(HEADS + 2):
        vector, matrix = soften(h - 1), products(h)
        running = True
        while running:
            running = next(matrix, done) is not done
            for _ in range(16):
                running = next(vector, done) is not done or running

    far_term = dot(far_grads[...], wkvt_ref[...]).astype(BF)
    far_rows[pl.ds(b * EXPD, EXPD)] = far_term.reshape(EXPD, BLOCK, D)

    @pl.when(b == pl.num_programs(0) - 1)
    def _():
        swap = swap_matrix()
        for u in range(0, far_ref.shape[1], 16):
            for g in range(0, BLOCK, 16):
                rows = far_rows[u : u + 16, g : g + 16, :].reshape(256, D)
                back_ref[g : g + 16, u : u + 16, :] = dot(swap, rows).astype(BF).reshape(16, 16, D)


def whole(*shape):
    return pl.BlockSpec(shape, lambda b: (0,) * len(shape), pipeline_mode=pl.Buffered(1))


def kept(*shape):
    return pl.BlockSpec(shape, lambda b: (0,) * len(shape))


def of_query(first, *shape):
    return pl.BlockSpec((1,) + shape, lambda b: (first + b,) + (0,) * len(shape))


def far_part(first, rel, live, sides, kvx, far, vkv, wkv, wkvt):
    count = rel.shape[0]
    listed = count * EXPD
    smem = pl.BlockSpec(memory_space=pltpu.SMEM)
    return pl.pallas_call(
        far_kernel,
        grid=(count,),
        in_specs=[
            smem,
            smem,
            of_query(first, HEADS, BLOCK, 2 * BLOCK),
            whole(count + 4, BLOCK, 2 * D),
            whole(BLOCK, listed, D),
            whole(VIRT, 2 * D),
            whole(D, 2 * D),
            whole(2 * D, D),
        ],
        out_specs=[
            kept(BLOCK, listed, D),
            of_query(0, HEADS, KEYS, 2 * BLOCK),
            of_query(0, KEYS, 2 * D),
        ],
        out_shape=[
            jax.ShapeDtypeStruct((BLOCK, listed, D), BF),
            jax.ShapeDtypeStruct((count, HEADS, KEYS, 2 * BLOCK), BF),
            jax.ShapeDtypeStruct((count, KEYS, 2 * D), BF),
        ],
        scratch_shapes=[
            pltpu.VMEM((listed, BLOCK, D), BF),
            pltpu.VMEM((EXPD * BLOCK, 2 * D), BF),
            pltpu.VMEM((KEYS, BLOCK), BF),
            pltpu.VMEM((BLOCK, 2 * BLOCK), BF),
            pltpu.VMEM((2, KEYS, 2 * BLOCK), F32),
        ],
        compiler_params=params(),
        cost_estimate=cost(count * 6_500_000_000, count * 7_000_000),
        name="far_part",
    )(rel, live, sides, kvx, far, vkv, wkv, wkvt)


def near_kernel(
    rel_ref, sides_ref, pairs_ref, kv_ref, wo_ref, mixed_ref, dq_ref, near_ref, near_grads, att, dqt
):
    b = pl.program_id(0)

    @pl.when(b == 0)
    def _():
        near_ref[...] = jnp.zeros_like(near_ref)

    for h in range(HEADS):
        rows = slice(h * HEAD, (h + 1) * HEAD)
        sums = dot(kv_ref[0, :, head_cols(h)], pairs_ref[0, h], TN)
        dqt[rows, :] = sums[:HEAD, :BLOCK]
        att[rows, :] = sums[HEAD:, BLOCK:]
        near_grads[:, head_cols(h)] = dot(pairs_ref[0, h, :NEAR, :], sides_ref[0, h], NT)
    for s in range(LOCD):
        near_ref[rel_ref[b, s]] += near_grads[s * BLOCK : (s + 1) * BLOCK, :]
    mixed_ref[0] = dot(att[...].T.astype(BF), wo_ref[...]).astype(BF)
    dq_ref[0] = (dqt[...] * HEAD**-0.5).T.astype(BF)


def near_part(first, rel, sides, pairs, kv, wo):
    count = rel.shape[0]
    return pl.pallas_call(
        near_kernel,
        grid=(count,),
        in_specs=[
            pl.BlockSpec(memory_space=pltpu.SMEM),
            of_query(first, HEADS, BLOCK, 2 * BLOCK),
            of_query(0, HEADS, KEYS, 2 * BLOCK),
            of_query(0, KEYS, 2 * D),
            whole(D, D),
        ],
        out_specs=[
            of_query(0, BLOCK, D),
            of_query(0, BLOCK, D),
            kept(count + 4, BLOCK, 2 * D),
        ],
        out_shape=[
            jax.ShapeDtypeStruct((count, BLOCK, D), BF),
            jax.ShapeDtypeStruct((count, BLOCK, D), BF),
            jax.ShapeDtypeStruct((count + 4, BLOCK, 2 * D), F32),
        ],
        scratch_shapes=[
            pltpu.VMEM((NEAR, 2 * D), F32),
            pltpu.VMEM((D, BLOCK), F32),
            pltpu.VMEM((D, BLOCK), F32),
        ],
        compiler_params=params(),
        cost_estimate=cost(count * 3_500_000_000, count * 7_000_000),
        name="near_part",
    )(rel, sides, pairs, kv, wo)


def exchange(rows):
    return lax.all_to_all(rows, AXES, split_axis=0, concat_axis=0, tiled=True)


def beside(low, high):
    up = [(i, i + 1) for i in range(NDEV - 1)]
    down = [(j, i) for i, j in up]
    return lax.ppermute(high, AXES, up), lax.ppermute(low, AXES, down)


def on_device(
    node_features,
    virtual_features,
    w_qkv,
    output_weight,
    block_home,
    local_blocks,
    expander_blocks,
    key_live,
    out_grad,
):
    me = lax.axis_index(AXES)
    x = node_features.reshape(BLK_DEV, BLOCK, D)
    grads = out_grad.reshape(BLK_DEV, BLOCK, D)
    stripes = exchange(stripe(x).reshape(NDEV, FOLD, WIDE)).reshape(NDEV * FOLD, WIDE)
    before, after = beside(x[:2], x[BLK_DEV - 2 :])

    w_kv = w_qkv[:, D:].reshape(D, 2, HEADS, HEAD).transpose(0, 2, 1, 3).reshape(D, 2 * D)
    w_kvt = w_kv.T
    w_qt = w_qkv[:, :D].T
    vkv = dot(virtual_features, w_kv).astype(BF)
    x_ext = jnp.concatenate([before, x, after], axis=0)

    graph = jnp.arange(NB, dtype=jnp.int32)

    def stored_at(ids, home):
        same = ids[..., None] == graph
        return jnp.sum(jnp.where(same, home, 0), axis=-1, dtype=jnp.int32)

    near_at = stored_at(local_blocks, block_home)
    rel = near_at - (me * BLK_DEV - 2)
    owner, inner = block_home // BLK_DEV, block_home % BLK_DEV
    code = owner * FOLD + jnp.where(inner < FOLD, inner, inner - FOLD + SPLIT)
    far_codes = stored_at(expander_blocks.reshape(NDEV, BLK_DEV * EXPD), code)
    codes = [far_codes[:, EXPD * f : EXPD * (f + n)].reshape(-1) for f, n in PARTS]
    tall = [c[:, None] for c in codes]
    stripes, x_ext, w_kv, w_kvt, w_qt, vkv, rel, tall, codes = lax.optimization_barrier(
        (stripes, x_ext, w_kv, w_kvt, w_qt, vkv, rel, tall, codes)
    )

    rows = pick_rows(tall[0], stripes)
    incoming = exchange(rows.reshape(NDEV, -1, D))
    later = pick_rows(tall[1], stripes)
    kvx = [project(x_ext, w_kv, f, n + 4) for f, n in PARTS]
    sides = make_sides(x, grads, w_qt, output_weight)
    incoming, later, kvx, sides = lax.optimization_barrier((incoming, later, kvx, sides))
    incoming = [incoming, exchange(later.reshape(NDEV, -1, D))]

    mixed, d_query, near, back = [], [], [], []
    for c, (first, count) in enumerate(PARTS):
        own = rel[first : first + count] - first
        live = key_live[first : first + count]
        far_back, pairs, kv = far_part(
            first, own, live, sides, kvx[c], incoming[c], vkv, w_kv, w_kvt
        )
        back.append(exchange(far_back).reshape(-1, D))
        m, dq, na = near_part(first, own, sides, pairs, kv, output_weight)
        if c == 0:
            incoming[1], m, dq, na = lax.optimization_barrier((incoming[1], m, dq, na))
        mixed.append(m)
        d_query.append(dq)
        near.append(na)

    ends = near[0][:2].astype(BF), near[-1][-2:].astype(BF)
    acc = add_rows(codes[0][None, :], back[0], (), F32)
    ends, acc, back[1] = lax.optimization_barrier((ends, acc, back[1]))
    low, high = beside(*ends)
    sums = []
    for c, (first, count) in enumerate(PARTS):
        total = near[c][2 : 2 + count]
        prior = low.astype(F32) if c == 0 else near[c - 1][-2:]
        nextp = high.astype(F32) if c == len(PARTS) - 1 else near[c + 1][:2]
        rest = jnp.zeros((count - 4, BLOCK, 2 * D), F32)
        sums.append(total + jnp.concatenate([prior, rest, nextp], axis=0))
    near_sum = jnp.concatenate(sums, axis=0).astype(BF).reshape(BLK_DEV * BLOCK, 2 * D)
    d_q = jnp.concatenate(d_query, axis=0).reshape(BLK_DEV * BLOCK, D)
    base = dot(d_q, w_qt) + dot(near_sum, w_kvt)

    far_sum = add_rows(codes[1][None, :], back[1], (acc,), BF)
    far = exchange(far_sum.reshape(NDEV, FOLD, WIDE)).reshape(NDEV * FOLD, WIDE)
    node_grad = finish(base.reshape(BLK_DEV, BLOCK, D), far)
    mixed = jnp.concatenate(mixed, axis=0).reshape(BLK_DEV * BLOCK, D)
    return mixed, node_grad.reshape(BLK_DEV * BLOCK, D)


def solution(mesh):
    rows = P(AXES, None)
    return jax.shard_map(
        on_device,
        mesh=mesh,
        in_specs=(rows, P(), P(), P(), P(), rows, P(), rows, rows),
        out_specs=(rows, rows),
        check_vma=False,
    )
```

```python
import jax
import jax.numpy as jnp
from jax import lax
from jax.experimental import pallas as pl
from jax.experimental.pallas import tpu as pltpu
from jax.sharding import PartitionSpec as P

HEADS = 8
HEAD = 64
BLOCK = 128
LOCD = 3
EXPD = 4
VIRT = 16
BLK_DEV = 12
D = 512
NB = 1536
NDEV = 128
FOLD = 8
WIDE = D + D // 2
HALF = D // 2
SPLIT = NDEV * FOLD
PARTS = ((0, 4), (4, 8))
NEAR = LOCD * BLOCK
LISTED = (LOCD + EXPD) * BLOCK
KEYS = LISTED + VIRT
AXES = ("group", "dev")
BF = jnp.bfloat16
F32 = jnp.float32
VMEM_LIMIT = 58 * 1024 * 1024
NT = (((1,), (1,)), ((), ()))
TN = (((0,), (0,)), ((), ()))


def dot(a, b, dims=None):
    if dims is None:
        return jnp.dot(a, b, preferred_element_type=F32)
    return lax.dot_general(a, b, dims, preferred_element_type=F32)


def params(limit=VMEM_LIMIT):
    return pltpu.CompilerParams(vmem_limit_bytes=limit)


def cost(flops, nbytes):
    return pl.CostEstimate(flops=flops, bytes_accessed=nbytes, transcendentals=0)


def swap_matrix():
    row = lax.broadcasted_iota(jnp.int32, (256, 256), 0)
    col = lax.broadcasted_iota(jnp.int32, (256, 256), 1)
    return jnp.where(col == (row % 16) * 16 + row // 16, 1.0, 0.0).astype(BF)


def fold_matrices(transposed):
    shape = (BLK_DEV * 16, 16 * FOLD) if transposed else (16 * FOLD, BLK_DEV * 16)
    folded = lax.broadcasted_iota(jnp.int32, shape, 1 if transposed else 0)
    plain = lax.broadcasted_iota(jnp.int32, shape, 0 if transposed else 1)
    same = folded // FOLD == plain % 16
    row, block = folded % FOLD, plain // 16
    return [
        jnp.where(same & hit, 1.0, 0.0).astype(BF)
        for hit in (block == row, (block == row + 8) & (row < 4), (block == row + 4) & (row >= 4))
    ]


def stripe_kernel(x_ref, out_ref):
    whole, left, right = fold_matrices(False)
    for g in range(x_ref.shape[1] // 16):
        rows = x_ref[:, 16 * g : 16 * g + 16, :].reshape(BLK_DEV * 16, D)
        part = slice(16 * FOLD * g, 16 * FOLD * (g + 1))
        out_ref[part, :D] = dot(whole, rows).astype(BF)
        out_ref[part, D:] = (dot(left, rows[:, :HALF]) + dot(right, rows[:, HALF:])).astype(BF)


def stripe(x):
    step = 64
    return pl.pallas_call(
        stripe_kernel,
        grid=(BLOCK // step,),
        in_specs=[pl.BlockSpec((BLK_DEV, step, D), lambda i: (0, i, 0))],
        out_specs=pl.BlockSpec((step * FOLD, WIDE), lambda i: (i, 0)),
        out_shape=jax.ShapeDtypeStruct((BLOCK * FOLD, WIDE), BF),
        compiler_params=params(),
        name="stripe",
    )(x)


def project_kernel(x_ref, w_ref, kv_ref):
    kv_ref[...] = dot(x_ref[...].reshape(4 * BLOCK, D), w_ref[...]).astype(BF).reshape(4, BLOCK, 2 * D)


def project(x_ext, w_kv, first, count):
    return pl.pallas_call(
        project_kernel,
        grid=(count // 4,),
        in_specs=[
            pl.BlockSpec((4, BLOCK, D), lambda i: (first // 4 + i, 0, 0)),
            pl.BlockSpec((D, 2 * D), lambda i: (0, 0)),
        ],
        out_specs=pl.BlockSpec((4, BLOCK, 2 * D), lambda i: (i, 0, 0)),
        out_shape=jax.ShapeDtypeStruct((count, BLOCK, 2 * D), BF),
        compiler_params=params(),
        cost_estimate=cost(count * 150_000_000, 12_000_000),
        name="project",
    )(x_ext, w_kv)


def sides_kernel(x_ref, grad_ref, wqt_ref, wo_ref, out_ref):
    out_ref[...] = jnp.zeros_like(out_ref)
    qt = (dot(wqt_ref[...], x_ref[...].reshape(-1, D), NT).astype(BF) * HEAD**-0.5).astype(BF)
    dat = dot(wo_ref[...], grad_ref[...].reshape(-1, D), NT).astype(BF)
    for i in range(x_ref.shape[0]):
        part = slice(i * BLOCK, (i + 1) * BLOCK)
        for h in range(HEADS):
            out_ref[i, h, :HEAD, :BLOCK] = qt[h * HEAD : (h + 1) * HEAD, part]
            out_ref[i, h, HEAD:, BLOCK:] = dat[h * HEAD : (h + 1) * HEAD, part]


def make_sides(x, grads, w_qt, wo, first, count):
    step = 4
    rows = pl.BlockSpec((step, BLOCK, D), lambda i: (first // step + i, 0, 0))
    weight = pl.BlockSpec((D, D), lambda i: (0, 0))
    return pl.pallas_call(
        sides_kernel,
        grid=(count // step,),
        in_specs=[rows, rows, weight, weight],
        out_specs=pl.BlockSpec((step, HEADS, BLOCK, 2 * BLOCK), lambda i: (i, 0, 0, 0)),
        out_shape=jax.ShapeDtypeStruct((count, HEADS, BLOCK, 2 * BLOCK), BF),
        compiler_params=params(),
        cost_estimate=cost(count * 150_000_000, count * 800_000),
        name="make_sides",
    )(x, grads, w_qt, wo)


def unfold_matrices(transposed):
    shape = (SPLIT, SPLIT // 2) if transposed else (SPLIT // 2, SPLIT)
    folded = lax.broadcasted_iota(jnp.int32, shape, 0 if transposed else 1)
    plain = lax.broadcasted_iota(jnp.int32, shape, 1 if transposed else 0)
    left = plain // 4 * FOLD + plain % 4
    return [jnp.where(folded == left + shift, 1.0, 0.0).astype(BF) for shift in (0, 4)]


def spread_kernel(codes_ref, out_ref):
    for i in range(codes_ref.shape[0]):
        row = jnp.broadcast_to(codes_ref[i : i + 1, :], (BLOCK, BLOCK))
        out_ref[i * BLOCK : (i + 1) * BLOCK, :] = row.T


def spread(codes):
    n = codes.shape[0]
    return pl.pallas_call(
        spread_kernel,
        out_shape=jax.ShapeDtypeStruct((n, BLOCK), jnp.int32),
        compiler_params=params(),
        name="spread",
    )(codes.reshape(n // BLOCK, BLOCK))


def pick_kernel(codes_ref, stripes_ref, out_ref, table):
    @pl.when(pl.program_id(0) == 0)
    def _():
        left, right = unfold_matrices(False)
        table[:SPLIT, :] = stripes_ref[:, :D]
        halves = stripes_ref[:, D:]
        table[SPLIT:, :HALF] = dot(left, halves).astype(BF)
        table[SPLIT:, HALF:] = dot(right, halves).astype(BF)

    codes = codes_ref[...]
    at = lax.broadcasted_iota(jnp.int32, codes.shape, 1)
    pick = [jnp.where(codes == at + k, 1.0, 0.0).astype(BF) for k in range(0, NB, BLOCK)]
    out_ref[...] = dot(jnp.concatenate(pick, axis=1), table[...]).astype(BF)


def pick_rows(codes, stripes):
    n = codes.shape[0]
    step = 512
    return pl.pallas_call(
        pick_kernel,
        grid=(n // step,),
        in_specs=[
            pl.BlockSpec((step, BLOCK), lambda i: (i, 0)),
            pl.BlockSpec((SPLIT, WIDE), lambda i: (0, 0)),
        ],
        out_specs=pl.BlockSpec((step, D), lambda i: (i, 0)),
        out_shape=jax.ShapeDtypeStruct((n, D), BF),
        scratch_shapes=[pltpu.VMEM((NB, D), BF)],
        compiler_params=params(),
        cost_estimate=cost(n * 2_100_000, 6_000_000),
        name="pick_rows",
    )(codes, stripes)


def add_kernel(codes_ref, rows_ref, out_ref):
    step, n = out_ref.shape[0], rows_ref.shape[0]
    at = lax.broadcasted_iota(jnp.int32, (step, n), 0) + pl.program_id(0) * step
    pick = jnp.where(codes_ref[...] == at, 1.0, 0.0).astype(BF)
    out_ref[...] = dot(pick, rows_ref[...])


def add_rows(codes, rows):
    n = rows.shape[0]
    step = 512
    return pl.pallas_call(
        add_kernel,
        grid=(NB // step,),
        in_specs=[
            pl.BlockSpec((1, n), lambda i: (0, 0)),
            pl.BlockSpec((n, D), lambda i: (0, 0)),
        ],
        out_specs=pl.BlockSpec((step, D), lambda i: (i, 0)),
        out_shape=jax.ShapeDtypeStruct((NB, D), F32),
        compiler_params=params(),
        cost_estimate=cost(n * 1_600_000, 8_000_000),
        name="add_rows",
    )(codes, rows)


def last_add_kernel(codes_ref, rows_ref, acc_ref, out_ref):
    step, n = acc_ref.shape[0], rows_ref.shape[0]
    at = lax.broadcasted_iota(jnp.int32, (step, n), 0) + pl.program_id(0) * step
    pick = jnp.where(codes_ref[...] == at, 1.0, 0.0).astype(BF)
    total = (acc_ref[...] + dot(pick, rows_ref[...])).astype(BF)
    for i in range(SPLIT // step):

        @pl.when(pl.program_id(0) == i)
        def _():
            out_ref[i * step : (i + 1) * step, :D] = total

    @pl.when(pl.program_id(0) == SPLIT // step)
    def _():
        left, right = unfold_matrices(True)
        out_ref[:, D:] = (dot(left, total[:, :HALF]) + dot(right, total[:, HALF:])).astype(BF)


def last_add_rows(codes, rows, acc):
    n = rows.shape[0]
    step = SPLIT // 2
    return pl.pallas_call(
        last_add_kernel,
        grid=(NB // step,),
        in_specs=[
            pl.BlockSpec((1, n), lambda i: (0, 0)),
            pl.BlockSpec((n, D), lambda i: (0, 0)),
            pl.BlockSpec((step, D), lambda i: (i, 0)),
        ],
        out_specs=pl.BlockSpec((SPLIT, WIDE), lambda i: (0, 0)),
        out_shape=jax.ShapeDtypeStruct((SPLIT, WIDE), BF),
        compiler_params=params(),
        cost_estimate=cost(n * 1_600_000, 8_000_000),
        name="last_add_rows",
    )(codes, rows, acc)


def finish_kernel(base_ref, far_ref, out_ref):
    whole, left, right = fold_matrices(True)
    for g in range(base_ref.shape[1] // 16):
        part = slice(16 * g, 16 * g + 16)
        rows = far_ref[16 * FOLD * g : 16 * FOLD * (g + 1)]
        main = dot(whole, rows[:, :D])
        halves = rows[:, D:]
        low = (main[:, :HALF] + dot(left, halves)).reshape(BLK_DEV, 16, HALF)
        high = (main[:, HALF:] + dot(right, halves)).reshape(BLK_DEV, 16, HALF)
        out_ref[:, part, :HALF] = (base_ref[:, part, :HALF] + low).astype(BF)
        out_ref[:, part, HALF:] = (base_ref[:, part, HALF:] + high).astype(BF)


def finish(base, far):
    step = 32
    rows = pl.BlockSpec((BLK_DEV, step, D), lambda i: (0, i, 0))
    return pl.pallas_call(
        finish_kernel,
        grid=(BLOCK // step,),
        in_specs=[rows, pl.BlockSpec((step * FOLD, WIDE), lambda i: (i, 0))],
        out_specs=rows,
        out_shape=jax.ShapeDtypeStruct((BLK_DEV, BLOCK, D), BF),
        compiler_params=params(),
        name="finish",
    )(base, far)


def scaled(side, inverse):
    both = jnp.concatenate([inverse, inverse], axis=1)
    return (side.astype(F32) * both).astype(BF)


def head_cols(h):
    return slice(h * 2 * HEAD, (h + 1) * 2 * HEAD)


def far_kernel(
    rel_ref,
    live_ref,
    sides_ref,
    kvx_ref,
    far_ref,
    vkv_ref,
    wkv_ref,
    wkvt_ref,
    back_ref,
    pairs_ref,
    kv_ref,
    inverse_ref,
    far_rows,
    far_grads,
    bias,
    ones,
    scores,
    d_probs,
    tops,
):
    b = pl.program_id(0)
    kv = kv_ref.at[0]

    @pl.when(b == 0)
    def _():
        bias[LISTED:KEYS, :] = jnp.zeros((VIRT, BLOCK), BF)
        lane = lax.broadcasted_iota(jnp.int32, (BLOCK, 2 * BLOCK), 1)
        row = lax.broadcasted_iota(jnp.int32, (BLOCK, 2 * BLOCK), 0)
        ones[...] = jnp.where((row == 0) & (lane < BLOCK), 1.0, 0.0).astype(BF)

    turn = lax.rem(b, 4)

    @pl.when(turn == 0)
    def _():
        swap = swap_matrix()
        for g in range(0, BLOCK, 16):
            rows = dot(swap, far_ref[g : g + 16].reshape(256, D)).astype(BF)
            far_rows[:, g : g + 16, :] = rows.reshape(16, 16, D)

    far_x = far_rows[pl.ds(turn * EXPD, EXPD)].reshape(EXPD * BLOCK, D)
    kv[NEAR:LISTED, :] = dot(far_x, wkv_ref[...]).astype(BF)
    kv[LISTED:KEYS, :] = vkv_ref[...]
    for s in range(LOCD):
        kv[s * BLOCK : (s + 1) * BLOCK, :] = kvx_ref[rel_ref[b, s]]
    key = lax.broadcasted_iota(jnp.int32, (BLOCK, BLOCK), 0)
    lane = lax.broadcasted_iota(jnp.int32, (BLOCK, BLOCK), 1)
    for s in range(LOCD + EXPD):
        part = slice(s * BLOCK, (s + 1) * BLOCK)
        closed = (key >= live_ref[b, s]) & (lane == 0)
        bias[part, :] = jnp.where(closed, -1e30, 0.0).astype(BF)

    def products(h):
        if h < HEADS:
            side = jnp.concatenate([sides_ref[0, h], ones[...]], axis=0)
            top = None
            for part in (slice(0, 464), slice(464, KEYS)):
                keys = jnp.concatenate([kv[part, head_cols(h)], bias[part, :]], axis=1)
                both = dot(keys, side)
                scores[h % 2, part, :] = both[:, :BLOCK]
                d_probs[h % 2, part, :] = both[:, BLOCK:].astype(BF)
                most = jnp.max(both[:, :BLOCK].reshape(-1, 8, BLOCK), axis=0)
                top = most if top is None else jnp.maximum(top, most)
                yield
            tops[h % 2] = top
        g = h - 2
        if g >= 0:
            inverse = inverse_ref[0, g : g + 1, :]
            side = scaled(sides_ref[0, g], inverse)
            far_grads[:, head_cols(g)] = dot(pairs_ref[0, g, NEAR:LISTED, :], side, NT).astype(BF)
            yield

    def soften(h):
        if h < 0 or h >= HEADS:
            return
        now, d_now = scores.at[h % 2], d_probs.at[h % 2]
        pair = pairs_ref.at[0, h]
        step = 48
        folded = (step // 8, 8, BLOCK)
        parts = [slice(r, r + step) for r in range(0, KEYS, step)]
        top = jnp.max(tops[h % 2], axis=0, keepdims=True)
        total = jnp.zeros((8, BLOCK), F32)
        drift = jnp.zeros((8, BLOCK), F32)
        for part in parts:
            weights = jnp.exp(now[part, :] - top)
            total += jnp.sum(weights.reshape(folded), axis=0)
            weights = weights.astype(BF)
            pair[part, BLOCK:] = weights
            moved = (weights * d_now[part, :]).astype(F32)
            drift += jnp.sum(moved.reshape(folded), axis=0)
            yield
        inverse = 1.0 / jnp.sum(total, axis=0, keepdims=True)
        inverse_ref[0, h : h + 1, :] = inverse
        delta = (jnp.sum(drift, axis=0, keepdims=True) * inverse).astype(BF)
        for part in parts:
            pair[part, :BLOCK] = pair[part, BLOCK:] * (d_now[part, :] - delta)
            yield

    done = object()
    for h in range(HEADS + 2):
        vector, matrix = soften(h - 1), products(h)
        running = True
        while running:
            running = next(matrix, done) is not done
            for _ in range(16):
                running = next(vector, done) is not done or running

    far_term = dot(far_grads[...], wkvt_ref[...]).astype(BF)
    far_rows[pl.ds(turn * EXPD, EXPD)] = far_term.reshape(EXPD, BLOCK, D)

    @pl.when(turn == 3)
    def _():
        swap = swap_matrix()
        for g in range(0, BLOCK, 16):
            rows = far_rows[:, g : g + 16, :].reshape(256, D)
            back_ref[g : g + 16] = dot(swap, rows).astype(BF).reshape(16, 16, D)


def whole(*shape):
    return pl.BlockSpec(shape, lambda b: (0,) * len(shape), pipeline_mode=pl.Buffered(1))


def kept(*shape):
    return pl.BlockSpec(shape, lambda b: (0,) * len(shape))


def of_query(first, *shape):
    return pl.BlockSpec((1,) + shape, lambda b: (first + b,) + (0,) * len(shape))


def far_part(rel, live, sides, kvx, far, vkv, wkv, wkvt):
    count = rel.shape[0]
    listed = count * EXPD
    fours = pl.BlockSpec((BLOCK, 16, D), lambda b: (0, b // 4, 0))
    smem = pl.BlockSpec(memory_space=pltpu.SMEM)
    return pl.pallas_call(
        far_kernel,
        grid=(count,),
        in_specs=[
            smem,
            smem,
            of_query(0, HEADS, BLOCK, 2 * BLOCK),
            whole(count + 4, BLOCK, 2 * D),
            fours,
            whole(VIRT, 2 * D),
            whole(D, 2 * D),
            whole(2 * D, D),
        ],
        out_specs=[
            fours,
            of_query(0, HEADS, KEYS, 2 * BLOCK),
            of_query(0, KEYS, 2 * D),
            of_query(0, HEADS, BLOCK),
        ],
        out_shape=[
            jax.ShapeDtypeStruct((BLOCK, listed, D), BF),
            jax.ShapeDtypeStruct((count, HEADS, KEYS, 2 * BLOCK), BF),
            jax.ShapeDtypeStruct((count, KEYS, 2 * D), BF),
            jax.ShapeDtypeStruct((count, HEADS, BLOCK), F32),
        ],
        scratch_shapes=[
            pltpu.VMEM((16, BLOCK, D), BF),
            pltpu.VMEM((EXPD * BLOCK, 2 * D), BF),
            pltpu.VMEM((KEYS, BLOCK), BF),
            pltpu.VMEM((BLOCK, 2 * BLOCK), BF),
            pltpu.VMEM((2, KEYS, BLOCK), F32),
            pltpu.VMEM((2, KEYS, BLOCK), BF),
            pltpu.VMEM((2, 8, BLOCK), F32),
        ],
        compiler_params=params(),
        cost_estimate=cost(count * 6_500_000_000, count * 7_000_000),
        name="far_part",
    )(rel, live, sides, kvx, far, vkv, wkv, wkvt)


def near_kernel(
    rel_ref, sides_ref, pairs_ref, kv_ref, inverse_ref, wo_ref, mixed_ref, dq_ref, near_ref, near_grads, att, dqt
):
    b = pl.program_id(0)

    @pl.when(b == 0)
    def _():
        near_ref[...] = jnp.zeros_like(near_ref)

    for h in range(HEADS):
        rows = slice(h * HEAD, (h + 1) * HEAD)
        sums = dot(kv_ref[0, :, head_cols(h)], pairs_ref[0, h], TN)
        inverse = inverse_ref[0, h : h + 1, :]
        dqt[rows, :] = sums[:HEAD, :BLOCK] * inverse
        att[rows, :] = sums[HEAD:, BLOCK:] * inverse
        side = scaled(sides_ref[0, h], inverse)
        near_grads[:, head_cols(h)] = dot(pairs_ref[0, h, :NEAR, :], side, NT)
    for s in range(LOCD):
        near_ref[rel_ref[b, s]] += near_grads[s * BLOCK : (s + 1) * BLOCK, :]
    mixed_ref[0] = dot(att[...].T.astype(BF), wo_ref[...]).astype(BF)
    dq_ref[0] = (dqt[...] * HEAD**-0.5).T.astype(BF)


def near_part(rel, sides, pairs, kv, inverse, wo):
    count = rel.shape[0]
    return pl.pallas_call(
        near_kernel,
        grid=(count,),
        in_specs=[
            pl.BlockSpec(memory_space=pltpu.SMEM),
            of_query(0, HEADS, BLOCK, 2 * BLOCK),
            of_query(0, HEADS, KEYS, 2 * BLOCK),
            of_query(0, KEYS, 2 * D),
            of_query(0, HEADS, BLOCK),
            whole(D, D),
        ],
        out_specs=[
            of_query(0, BLOCK, D),
            of_query(0, BLOCK, D),
            kept(count + 4, BLOCK, 2 * D),
        ],
        out_shape=[
            jax.ShapeDtypeStruct((count, BLOCK, D), BF),
            jax.ShapeDtypeStruct((count, BLOCK, D), BF),
            jax.ShapeDtypeStruct((count + 4, BLOCK, 2 * D), F32),
        ],
        scratch_shapes=[
            pltpu.VMEM((NEAR, 2 * D), F32),
            pltpu.VMEM((D, BLOCK), F32),
            pltpu.VMEM((D, BLOCK), F32),
        ],
        compiler_params=params(),
        cost_estimate=cost(count * 3_500_000_000, count * 7_000_000),
        name="near_part",
    )(rel, sides, pairs, kv, inverse, wo)


def exchange(rows):
    return lax.all_to_all(rows, AXES, split_axis=0, concat_axis=0, tiled=True)


def beside(low, high):
    up = [(i, i + 1) for i in range(NDEV - 1)]
    down = [(j, i) for i, j in up]
    return lax.ppermute(high, AXES, up), lax.ppermute(low, AXES, down)


def on_device(
    node_features,
    virtual_features,
    w_qkv,
    output_weight,
    block_home,
    local_blocks,
    expander_blocks,
    key_live,
    out_grad,
):
    me = lax.axis_index(AXES)
    x = node_features.reshape(BLK_DEV, BLOCK, D)
    grads = out_grad.reshape(BLK_DEV, BLOCK, D)
    striped = stripe(x)
    stripes = exchange(striped.reshape(NDEV, FOLD, WIDE)).reshape(NDEV * FOLD, WIDE)

    w_kv = w_qkv[:, D:].reshape(D, 2, HEADS, HEAD).transpose(0, 2, 1, 3).reshape(D, 2 * D)
    w_kvt = w_kv.T
    w_qt = w_qkv[:, :D].T
    vkv = dot(virtual_features, w_kv).astype(BF)

    graph = jnp.arange(NB, dtype=jnp.int32)

    def stored_at(ids, home):
        same = ids[..., None] == graph
        return jnp.sum(jnp.where(same, home, 0), axis=-1, dtype=jnp.int32)

    near_at = stored_at(local_blocks, block_home)
    rel = near_at - (me * BLK_DEV - 2)
    owner, inner = block_home // BLK_DEV, block_home % BLK_DEV
    code = jnp.where(inner < FOLD, owner * FOLD + inner, SPLIT + owner * 4 + inner - FOLD)
    far_codes = stored_at(expander_blocks.reshape(NDEV, BLK_DEV * EXPD), code)
    low_x, high_x, far_codes = lax.optimization_barrier((x[:2], x[BLK_DEV - 2 :], far_codes))
    before, after = beside(low_x, high_x)
    codes = [far_codes[:, EXPD * f : EXPD * (f + n)].reshape(-1) for f, n in PARTS]
    tall = spread(codes[0])
    stripes, before, after, w_kv, w_kvt, w_qt, vkv, rel, tall, codes = lax.optimization_barrier(
        (stripes, before, after, w_kv, w_kvt, w_qt, vkv, rel, tall, codes)
    )

    rows = pick_rows(tall, stripes)
    incoming = exchange(rows.reshape(NDEV, -1, D))
    later = pick_rows(spread(codes[1]), stripes)
    x_ext = jnp.concatenate([before, x, after], axis=0)

    def prepared(first, count):
        kvx = project(x_ext, w_kv, first, count + 4)
        return kvx, make_sides(x, grads, w_qt, output_weight, first, count)

    ready = prepared(*PARTS[0])
    incoming, later, ready, x_ext = lax.optimization_barrier((incoming, later, ready, x_ext))
    incoming = [incoming, exchange(later.reshape(NDEV, -1, D))]

    mixed, d_query, near, back = [], [], [], []
    for c, (first, count) in enumerate(PARTS):
        own = rel[first : first + count] - first
        live = key_live[first : first + count]
        kvx, sides = ready
        far_back, pairs, kv, inverse = far_part(
            own, live, sides, kvx, incoming[c], vkv, w_kv, w_kvt
        )
        back.append(exchange(far_back).reshape(-1, D))
        m, dq, na = near_part(own, sides, pairs, kv, inverse, output_weight)
        if c == 0:
            ready = prepared(*PARTS[1])
            incoming[1], m, dq, na, ready = lax.optimization_barrier(
                (incoming[1], m, dq, na, ready)
            )
        mixed.append(m)
        d_query.append(dq)
        near.append(na)

    acc = add_rows(codes[0][None, :], back[0])
    low, high = beside(near[0][:2].astype(BF), near[-1][-2:].astype(BF))
    low, high, acc, back[1] = lax.optimization_barrier((low, high, acc, back[1]))
    sums = []
    for c, (first, count) in enumerate(PARTS):
        total = near[c][2 : 2 + count]
        prior = low.astype(F32) if c == 0 else near[c - 1][-2:]
        nextp = high.astype(F32) if c == len(PARTS) - 1 else near[c + 1][:2]
        rest = jnp.zeros((count - 4, BLOCK, 2 * D), F32)
        sums.append(total + jnp.concatenate([prior, rest, nextp], axis=0))
    near_sum = jnp.concatenate(sums, axis=0).astype(BF).reshape(BLK_DEV * BLOCK, 2 * D)
    d_q = jnp.concatenate(d_query, axis=0).reshape(BLK_DEV * BLOCK, D)
    base = dot(d_q, w_qt) + dot(near_sum, w_kvt)

    far_sum = last_add_rows(codes[1][None, :], back[1], acc)
    far = exchange(far_sum.reshape(NDEV, FOLD, WIDE)).reshape(NDEV * FOLD, WIDE)
    node_grad = finish(base.reshape(BLK_DEV, BLOCK, D), far)
    mixed = jnp.concatenate(mixed, axis=0).reshape(BLK_DEV * BLOCK, D)
    return mixed, node_grad.reshape(BLK_DEV * BLOCK, D)


def solution(mesh):
    rows = P(AXES, None)
    return jax.shard_map(
        on_device,
        mesh=mesh,
        in_specs=(rows, P(), P(), P(), P(), rows, P(), rows, rows),
        out_specs=(rows, rows),
        check_vma=False,
    )
```

```python
import jax
import jax.numpy as jnp
from jax import lax
from jax.experimental import pallas as pl
from jax.experimental.pallas import tpu as pltpu
from jax.sharding import PartitionSpec as P

HEADS = 8
HEAD = 64
BLOCK = 128
LOCD = 3
EXPD = 4
VIRT = 16
BLK_DEV = 12
D = 512
NB = 1536
NDEV = 128
FOLD = 8
WIDE = D + D // 2
HALF = D // 2
SPLIT = NDEV * FOLD
PARTS = ((0, 4), (4, 8))
NEAR = LOCD * BLOCK
LISTED = (LOCD + EXPD) * BLOCK
KEYS = LISTED + VIRT
AXES = ("group", "dev")
BF = jnp.bfloat16
F32 = jnp.float32
NT = (((1,), (1,)), ((), ()))
TN = (((0,), (0,)), ((), ()))


def dot(a, b, dims=None):
    if dims is None:
        return jnp.dot(a, b, preferred_element_type=F32)
    return lax.dot_general(a, b, dims, preferred_element_type=F32)


def params(mib):
    return pltpu.CompilerParams(vmem_limit_bytes=mib * 1024 * 1024)


def cost(flops, nbytes):
    return pl.CostEstimate(flops=flops, bytes_accessed=nbytes, transcendentals=0)


def swap_matrix():
    row = lax.broadcasted_iota(jnp.int32, (256, 256), 0)
    col = lax.broadcasted_iota(jnp.int32, (256, 256), 1)
    return jnp.where(col == (row % 16) * 16 + row // 16, 1.0, 0.0).astype(BF)


def fold_matrices(transposed):
    shape = (BLK_DEV * 16, 16 * FOLD) if transposed else (16 * FOLD, BLK_DEV * 16)
    folded = lax.broadcasted_iota(jnp.int32, shape, 1 if transposed else 0)
    plain = lax.broadcasted_iota(jnp.int32, shape, 0 if transposed else 1)
    same = folded // FOLD == plain % 16
    row, block = folded % FOLD, plain // 16
    return [
        jnp.where(same & hit, 1.0, 0.0).astype(BF)
        for hit in (block == row, (block == row + 8) & (row < 4), (block == row + 4) & (row >= 4))
    ]


def stripe_kernel(x_ref, out_ref):
    whole, left, right = fold_matrices(False)
    for g in range(x_ref.shape[1] // 16):
        rows = x_ref[:, 16 * g : 16 * g + 16, :].reshape(BLK_DEV * 16, D)
        part = slice(16 * FOLD * g, 16 * FOLD * (g + 1))
        out_ref[part, :D] = dot(whole, rows).astype(BF)
        out_ref[part, D:] = (dot(left, rows[:, :HALF]) + dot(right, rows[:, HALF:])).astype(BF)


def stripe(x):
    step = 64
    return pl.pallas_call(
        stripe_kernel,
        grid=(BLOCK // step,),
        in_specs=[pl.BlockSpec((BLK_DEV, step, D), lambda i: (0, i, 0))],
        out_specs=pl.BlockSpec((step * FOLD, WIDE), lambda i: (i, 0)),
        out_shape=jax.ShapeDtypeStruct((BLOCK * FOLD, WIDE), BF),
        compiler_params=params(58),
        name="stripe",
    )(x)


def project_kernel(x_ref, w_ref, kv_ref):
    kv_ref[...] = dot(x_ref[...].reshape(4 * BLOCK, D), w_ref[...]).astype(BF).reshape(4, BLOCK, 2 * D)


def project(x_ext, w_kv, first, count):
    return pl.pallas_call(
        project_kernel,
        grid=(count // 4,),
        in_specs=[
            pl.BlockSpec((4, BLOCK, D), lambda i: (first // 4 + i, 0, 0)),
            pl.BlockSpec((D, 2 * D), lambda i: (0, 0)),
        ],
        out_specs=pl.BlockSpec((4, BLOCK, 2 * D), lambda i: (i, 0, 0)),
        out_shape=jax.ShapeDtypeStruct((count, BLOCK, 2 * D), BF),
        compiler_params=params(20),
        cost_estimate=cost(count * 150_000_000, 12_000_000),
        name="project",
    )(x_ext, w_kv)


def sides_kernel(x_ref, grad_ref, wqt_ref, wo_ref, out_ref):
    out_ref[...] = jnp.zeros_like(out_ref)
    qt = (dot(wqt_ref[...], x_ref[...].reshape(-1, D), NT).astype(BF) * HEAD**-0.5).astype(BF)
    dat = dot(wo_ref[...], grad_ref[...].reshape(-1, D), NT).astype(BF)
    for i in range(x_ref.shape[0]):
        part = slice(i * BLOCK, (i + 1) * BLOCK)
        for h in range(HEADS):
            out_ref[i, h, :HEAD, :BLOCK] = qt[h * HEAD : (h + 1) * HEAD, part]
            out_ref[i, h, HEAD:, BLOCK:] = dat[h * HEAD : (h + 1) * HEAD, part]


def make_sides(x, grads, w_qt, wo, first, count):
    step = 4
    rows = pl.BlockSpec((step, BLOCK, D), lambda i: (first // step + i, 0, 0))
    weight = pl.BlockSpec((D, D), lambda i: (0, 0))
    return pl.pallas_call(
        sides_kernel,
        grid=(count // step,),
        in_specs=[rows, rows, weight, weight],
        out_specs=pl.BlockSpec((step, HEADS, BLOCK, 2 * BLOCK), lambda i: (i, 0, 0, 0)),
        out_shape=jax.ShapeDtypeStruct((count, HEADS, BLOCK, 2 * BLOCK), BF),
        compiler_params=params(20),
        cost_estimate=cost(count * 150_000_000, count * 800_000),
        name="make_sides",
    )(x, grads, w_qt, wo)


def unfold_matrices(transposed):
    shape = (SPLIT, SPLIT // 2) if transposed else (SPLIT // 2, SPLIT)
    folded = lax.broadcasted_iota(jnp.int32, shape, 0 if transposed else 1)
    plain = lax.broadcasted_iota(jnp.int32, shape, 1 if transposed else 0)
    left = plain // 4 * FOLD + plain % 4
    return [jnp.where(folded == left + shift, 1.0, 0.0).astype(BF) for shift in (0, 4)]


def spread_kernel(codes_ref, out_ref):
    for i in range(codes_ref.shape[0]):
        row = jnp.broadcast_to(codes_ref[i : i + 1, :], (BLOCK, BLOCK))
        out_ref[i * BLOCK : (i + 1) * BLOCK, :] = row.T


def spread(codes):
    n = codes.shape[0]
    return pl.pallas_call(
        spread_kernel,
        out_shape=jax.ShapeDtypeStruct((n, BLOCK), jnp.int32),
        compiler_params=params(8),
        name="spread",
    )(codes.reshape(n // BLOCK, BLOCK))


def pick_kernel(codes_ref, stripes_ref, out_ref, table):
    @pl.when(pl.program_id(0) == 0)
    def _():
        left, right = unfold_matrices(False)
        table[:SPLIT, :] = stripes_ref[:, :D]
        halves = stripes_ref[:, D:]
        table[SPLIT:, :HALF] = dot(left, halves).astype(BF)
        table[SPLIT:, HALF:] = dot(right, halves).astype(BF)

    codes = codes_ref[...]
    at = lax.broadcasted_iota(jnp.int32, codes.shape, 1)
    pick = [jnp.where(codes == at + k, 1.0, 0.0).astype(BF) for k in range(0, NB, BLOCK)]
    out_ref[...] = dot(jnp.concatenate(pick, axis=1), table[...]).astype(BF)


def pick_rows(codes, stripes):
    n = codes.shape[0]
    step = 512
    return pl.pallas_call(
        pick_kernel,
        grid=(n // step,),
        in_specs=[
            pl.BlockSpec((step, BLOCK), lambda i: (i, 0)),
            pl.BlockSpec((SPLIT, WIDE), lambda i: (0, 0)),
        ],
        out_specs=pl.BlockSpec((step, D), lambda i: (i, 0)),
        out_shape=jax.ShapeDtypeStruct((n, D), BF),
        scratch_shapes=[pltpu.VMEM((NB, D), BF)],
        compiler_params=params(58),
        cost_estimate=cost(n * 2_100_000, 6_000_000),
        name="pick_rows",
    )(codes, stripes)


def add_kernel(codes_ref, rows_ref, out_ref):
    step, n = out_ref.shape[0], rows_ref.shape[0]
    at = lax.broadcasted_iota(jnp.int32, (step, n), 0) + pl.program_id(0) * step
    pick = jnp.where(codes_ref[...] == at, 1.0, 0.0).astype(BF)
    out_ref[...] = dot(pick, rows_ref[...])


def add_rows(codes, rows):
    n = rows.shape[0]
    step = 512
    return pl.pallas_call(
        add_kernel,
        grid=(NB // step,),
        in_specs=[
            pl.BlockSpec((1, n), lambda i: (0, 0)),
            pl.BlockSpec((n, D), lambda i: (0, 0)),
        ],
        out_specs=pl.BlockSpec((step, D), lambda i: (i, 0)),
        out_shape=jax.ShapeDtypeStruct((NB, D), F32),
        compiler_params=params(40),
        cost_estimate=cost(n * 1_600_000, 8_000_000),
        name="add_rows",
    )(codes, rows)


def last_add_kernel(codes_ref, rows_ref, acc_ref, out_ref):
    step, n = acc_ref.shape[0], rows_ref.shape[0]
    at = lax.broadcasted_iota(jnp.int32, (step, n), 0) + pl.program_id(0) * step
    pick = jnp.where(codes_ref[...] == at, 1.0, 0.0).astype(BF)
    total = (acc_ref[...] + dot(pick, rows_ref[...])).astype(BF)
    for i in range(SPLIT // step):

        @pl.when(pl.program_id(0) == i)
        def _():
            out_ref[i * step : (i + 1) * step, :D] = total

    @pl.when(pl.program_id(0) == SPLIT // step)
    def _():
        left, right = unfold_matrices(True)
        out_ref[:, D:] = (dot(left, total[:, :HALF]) + dot(right, total[:, HALF:])).astype(BF)


def last_add_rows(codes, rows, acc):
    n = rows.shape[0]
    step = SPLIT // 2
    return pl.pallas_call(
        last_add_kernel,
        grid=(NB // step,),
        in_specs=[
            pl.BlockSpec((1, n), lambda i: (0, 0)),
            pl.BlockSpec((n, D), lambda i: (0, 0)),
            pl.BlockSpec((step, D), lambda i: (i, 0)),
        ],
        out_specs=pl.BlockSpec((SPLIT, WIDE), lambda i: (0, 0)),
        out_shape=jax.ShapeDtypeStruct((SPLIT, WIDE), BF),
        compiler_params=params(58),
        cost_estimate=cost(n * 1_600_000, 8_000_000),
        name="last_add_rows",
    )(codes, rows, acc)


def finish_kernel(base_ref, far_ref, out_ref):
    whole, left, right = fold_matrices(True)
    for g in range(base_ref.shape[1] // 16):
        part = slice(16 * g, 16 * g + 16)
        rows = far_ref[16 * FOLD * g : 16 * FOLD * (g + 1)]
        main = dot(whole, rows[:, :D])
        halves = rows[:, D:]
        low = (main[:, :HALF] + dot(left, halves)).reshape(BLK_DEV, 16, HALF)
        high = (main[:, HALF:] + dot(right, halves)).reshape(BLK_DEV, 16, HALF)
        out_ref[:, part, :HALF] = (base_ref[:, part, :HALF] + low).astype(BF)
        out_ref[:, part, HALF:] = (base_ref[:, part, HALF:] + high).astype(BF)


def finish(base, far):
    step = 32
    rows = pl.BlockSpec((BLK_DEV, step, D), lambda i: (0, i, 0))
    return pl.pallas_call(
        finish_kernel,
        grid=(BLOCK // step,),
        in_specs=[rows, pl.BlockSpec((step * FOLD, WIDE), lambda i: (i, 0))],
        out_specs=rows,
        out_shape=jax.ShapeDtypeStruct((BLK_DEV, BLOCK, D), BF),
        compiler_params=params(16),
        name="finish",
    )(base, far)


def scaled(side, inverse):
    both = jnp.concatenate([inverse, inverse], axis=1)
    return (side.astype(F32) * both).astype(BF)


def head_cols(h):
    return slice(h * 2 * HEAD, (h + 1) * 2 * HEAD)


def far_kernel(
    rel_ref,
    live_ref,
    sides_ref,
    kvx_ref,
    far_ref,
    vkv_ref,
    wkv_ref,
    wkvt_ref,
    back_ref,
    pairs_ref,
    kv_ref,
    inverse_ref,
    far_rows,
    far_grads,
    bias,
    ones,
    scores,
    d_probs,
    tops,
):
    b = pl.program_id(0)
    kv = kv_ref.at[0]

    @pl.when(b == 0)
    def _():
        bias[LISTED:KEYS, :] = jnp.zeros((VIRT, BLOCK), BF)
        lane = lax.broadcasted_iota(jnp.int32, (BLOCK, 2 * BLOCK), 1)
        row = lax.broadcasted_iota(jnp.int32, (BLOCK, 2 * BLOCK), 0)
        ones[...] = jnp.where((row == 0) & (lane < BLOCK), 1.0, 0.0).astype(BF)

    turn = lax.rem(b, 4)

    @pl.when(turn == 0)
    def _():
        swap = swap_matrix()
        for g in range(0, BLOCK, 16):
            rows = dot(swap, far_ref[g : g + 16].reshape(256, D)).astype(BF)
            far_rows[:, g : g + 16, :] = rows.reshape(16, 16, D)

    far_x = far_rows[pl.ds(turn * EXPD, EXPD)].reshape(EXPD * BLOCK, D)
    kv[NEAR:LISTED, :] = dot(far_x, wkv_ref[...]).astype(BF)
    kv[LISTED:KEYS, :] = vkv_ref[...]
    for s in range(LOCD):
        kv[s * BLOCK : (s + 1) * BLOCK, :] = kvx_ref[rel_ref[b, s]]
    key = lax.broadcasted_iota(jnp.int32, (BLOCK, BLOCK), 0)
    lane = lax.broadcasted_iota(jnp.int32, (BLOCK, BLOCK), 1)
    for s in range(LOCD + EXPD):
        part = slice(s * BLOCK, (s + 1) * BLOCK)
        closed = (key >= live_ref[b, s]) & (lane == 0)
        bias[part, :] = jnp.where(closed, -1e30, 0.0).astype(BF)

    def products(h):
        if h < HEADS:
            side = jnp.concatenate([sides_ref[0, h], ones[...]], axis=0)
            top = None
            for part in (slice(0, 464), slice(464, KEYS)):
                keys = jnp.concatenate([kv[part, head_cols(h)], bias[part, :]], axis=1)
                both = dot(keys, side)
                scores[h % 2, part, :] = both[:, :BLOCK]
                d_probs[h % 2, part, :] = both[:, BLOCK:].astype(BF)
                most = jnp.max(both[:, :BLOCK].reshape(-1, 8, BLOCK), axis=0)
                top = most if top is None else jnp.maximum(top, most)
                yield
            tops[h % 2] = top
        g = h - 2
        if g >= 0:
            inverse = inverse_ref[0, g : g + 1, :]
            side = scaled(sides_ref[0, g], inverse)
            far_grads[:, head_cols(g)] = dot(pairs_ref[0, g, NEAR:LISTED, :], side, NT).astype(BF)
            yield

    def soften(h):
        if h < 0 or h >= HEADS:
            return
        now, d_now = scores.at[h % 2], d_probs.at[h % 2]
        pair = pairs_ref.at[0, h]
        step = 48
        folded = (step // 8, 8, BLOCK)
        parts = [slice(r, r + step) for r in range(0, KEYS, step)]
        top = jnp.max(tops[h % 2], axis=0, keepdims=True)
        total = jnp.zeros((8, BLOCK), F32)
        drift = jnp.zeros((8, BLOCK), F32)
        for part in parts:
            weights = jnp.exp(now[part, :] - top)
            total += jnp.sum(weights.reshape(folded), axis=0)
            weights = weights.astype(BF)
            pair[part, BLOCK:] = weights
            moved = (weights * d_now[part, :]).astype(F32)
            drift += jnp.sum(moved.reshape(folded), axis=0)
            yield
        inverse = 1.0 / jnp.sum(total, axis=0, keepdims=True)
        inverse_ref[0, h : h + 1, :] = inverse
        delta = (jnp.sum(drift, axis=0, keepdims=True) * inverse).astype(BF)
        for part in parts:
            pair[part, :BLOCK] = pair[part, BLOCK:] * (d_now[part, :] - delta)
            yield

    done = object()
    for h in range(HEADS + 2):
        vector, matrix = soften(h - 1), products(h)
        running = True
        while running:
            running = next(matrix, done) is not done
            for _ in range(16):
                running = next(vector, done) is not done or running

    far_term = dot(far_grads[...], wkvt_ref[...]).astype(BF)
    far_rows[pl.ds(turn * EXPD, EXPD)] = far_term.reshape(EXPD, BLOCK, D)

    @pl.when(turn == 3)
    def _():
        swap = swap_matrix()
        for g in range(0, BLOCK, 16):
            rows = far_rows[:, g : g + 16, :].reshape(256, D)
            back_ref[g : g + 16] = dot(swap, rows).astype(BF).reshape(16, 16, D)


def whole(*shape):
    return pl.BlockSpec(shape, lambda b: (0,) * len(shape), pipeline_mode=pl.Buffered(1))


def kept(*shape):
    return pl.BlockSpec(shape, lambda b: (0,) * len(shape))


def of_query(first, *shape):
    return pl.BlockSpec((1,) + shape, lambda b: (first + b,) + (0,) * len(shape))


def far_part(rel, live, sides, kvx, far, vkv, wkv, wkvt):
    count = rel.shape[0]
    listed = count * EXPD
    fours = pl.BlockSpec((BLOCK, 16, D), lambda b: (0, b // 4, 0))
    smem = pl.BlockSpec(memory_space=pltpu.SMEM)
    return pl.pallas_call(
        far_kernel,
        grid=(count,),
        in_specs=[
            smem,
            smem,
            of_query(0, HEADS, BLOCK, 2 * BLOCK),
            whole(count + 4, BLOCK, 2 * D),
            fours,
            whole(VIRT, 2 * D),
            whole(D, 2 * D),
            whole(2 * D, D),
        ],
        out_specs=[
            fours,
            of_query(0, HEADS, KEYS, 2 * BLOCK),
            of_query(0, KEYS, 2 * D),
            of_query(0, HEADS, BLOCK),
        ],
        out_shape=[
            jax.ShapeDtypeStruct((BLOCK, listed, D), BF),
            jax.ShapeDtypeStruct((count, HEADS, KEYS, 2 * BLOCK), BF),
            jax.ShapeDtypeStruct((count, KEYS, 2 * D), BF),
            jax.ShapeDtypeStruct((count, HEADS, BLOCK), F32),
        ],
        scratch_shapes=[
            pltpu.VMEM((16, BLOCK, D), BF),
            pltpu.VMEM((EXPD * BLOCK, 2 * D), BF),
            pltpu.VMEM((KEYS, BLOCK), BF),
            pltpu.VMEM((BLOCK, 2 * BLOCK), BF),
            pltpu.VMEM((2, KEYS, BLOCK), F32),
            pltpu.VMEM((2, KEYS, BLOCK), BF),
            pltpu.VMEM((2, 8, BLOCK), F32),
        ],
        compiler_params=params(46),
        cost_estimate=cost(count * 6_500_000_000, count * 7_000_000),
        name="far_part",
    )(rel, live, sides, kvx, far, vkv, wkv, wkvt)


def near_kernel(
    rel_ref, sides_ref, pairs_ref, kv_ref, inverse_ref, wo_ref, mixed_ref, dq_ref, near_ref, near_grads, att, dqt
):
    b = pl.program_id(0)

    @pl.when(b == 0)
    def _():
        near_ref[...] = jnp.zeros_like(near_ref)

    for h in range(HEADS):
        rows = slice(h * HEAD, (h + 1) * HEAD)
        sums = dot(kv_ref[0, :, head_cols(h)], pairs_ref[0, h], TN)
        inverse = inverse_ref[0, h : h + 1, :]
        dqt[rows, :] = sums[:HEAD, :BLOCK] * inverse
        att[rows, :] = sums[HEAD:, BLOCK:] * inverse
        side = scaled(sides_ref[0, h], inverse)
        near_grads[:, head_cols(h)] = dot(pairs_ref[0, h, :NEAR, :], side, NT)
    for s in range(LOCD):
        near_ref[rel_ref[b, s]] += near_grads[s * BLOCK : (s + 1) * BLOCK, :]
    mixed_ref[0] = dot(att[...].T.astype(BF), wo_ref[...]).astype(BF)
    dq_ref[0] = (dqt[...] * HEAD**-0.5).T.astype(BF)


def near_part(rel, sides, pairs, kv, inverse, wo):
    count = rel.shape[0]
    return pl.pallas_call(
        near_kernel,
        grid=(count,),
        in_specs=[
            pl.BlockSpec(memory_space=pltpu.SMEM),
            of_query(0, HEADS, BLOCK, 2 * BLOCK),
            of_query(0, HEADS, KEYS, 2 * BLOCK),
            of_query(0, KEYS, 2 * D),
            of_query(0, HEADS, BLOCK),
            whole(D, D),
        ],
        out_specs=[
            of_query(0, BLOCK, D),
            of_query(0, BLOCK, D),
            kept(count + 4, BLOCK, 2 * D),
        ],
        out_shape=[
            jax.ShapeDtypeStruct((count, BLOCK, D), BF),
            jax.ShapeDtypeStruct((count, BLOCK, D), BF),
            jax.ShapeDtypeStruct((count + 4, BLOCK, 2 * D), F32),
        ],
        scratch_shapes=[
            pltpu.VMEM((NEAR, 2 * D), F32),
            pltpu.VMEM((D, BLOCK), F32),
            pltpu.VMEM((D, BLOCK), F32),
        ],
        compiler_params=params(34),
        cost_estimate=cost(count * 3_500_000_000, count * 7_000_000),
        name="near_part",
    )(rel, sides, pairs, kv, inverse, wo)


def exchange(rows):
    return lax.all_to_all(rows, AXES, split_axis=0, concat_axis=0, tiled=True)


def beside(low, high):
    up = [(i, i + 1) for i in range(NDEV - 1)]
    down = [(j, i) for i, j in up]
    return lax.ppermute(high, AXES, up), lax.ppermute(low, AXES, down)


def on_device(
    node_features,
    virtual_features,
    w_qkv,
    output_weight,
    block_home,
    local_blocks,
    expander_blocks,
    key_live,
    out_grad,
):
    me = lax.axis_index(AXES)
    x = node_features.reshape(BLK_DEV, BLOCK, D)
    grads = out_grad.reshape(BLK_DEV, BLOCK, D)
    striped = stripe(x)
    stripes = exchange(striped.reshape(NDEV, FOLD, WIDE)).reshape(NDEV * FOLD, WIDE)

    w_kv = w_qkv[:, D:].reshape(D, 2, HEADS, HEAD).transpose(0, 2, 1, 3).reshape(D, 2 * D)
    w_kvt = w_kv.T
    w_qt = w_qkv[:, :D].T
    vkv = dot(virtual_features, w_kv).astype(BF)

    graph = jnp.arange(NB, dtype=jnp.int32)

    def stored_at(ids, home):
        same = ids[..., None] == graph
        return jnp.sum(jnp.where(same, home, 0), axis=-1, dtype=jnp.int32)

    near_at = stored_at(local_blocks, block_home)
    rel = near_at - (me * BLK_DEV - 2)
    owner, inner = block_home // BLK_DEV, block_home % BLK_DEV
    code = jnp.where(inner < FOLD, owner * FOLD + inner, SPLIT + owner * 4 + inner - FOLD)
    far_codes = stored_at(expander_blocks.reshape(NDEV, BLK_DEV * EXPD), code)
    low_x, high_x, far_codes = lax.optimization_barrier((x[:2], x[BLK_DEV - 2 :], far_codes))
    before, after = beside(low_x, high_x)
    codes = [far_codes[:, EXPD * f : EXPD * (f + n)].reshape(-1) for f, n in PARTS]
    tall = spread(codes[0])
    stripes, before, after, w_kv, w_kvt, w_qt, vkv, rel, tall, codes = lax.optimization_barrier(
        (stripes, before, after, w_kv, w_kvt, w_qt, vkv, rel, tall, codes)
    )

    rows = pick_rows(tall, stripes)
    incoming = exchange(rows.reshape(NDEV, -1, D))
    later = pick_rows(spread(codes[1]), stripes)
    x_ext = jnp.concatenate([before, x, after], axis=0)

    def prepared(first, count):
        kvx = project(x_ext, w_kv, first, count + 4)
        return kvx, make_sides(x, grads, w_qt, output_weight, first, count)

    ready = prepared(*PARTS[0])
    incoming, later, ready, x_ext = lax.optimization_barrier((incoming, later, ready, x_ext))
    incoming = [incoming, exchange(later.reshape(NDEV, -1, D))]

    mixed, d_query, near, back = [], [], [], []
    for c, (first, count) in enumerate(PARTS):
        own = rel[first : first + count] - first
        live = key_live[first : first + count]
        kvx, sides = ready
        far_back, pairs, kv, inverse = far_part(
            own, live, sides, kvx, incoming[c], vkv, w_kv, w_kvt
        )
        back.append(exchange(far_back).reshape(-1, D))
        m, dq, na = near_part(own, sides, pairs, kv, inverse, output_weight)
        if c == 0:
            ready = prepared(*PARTS[1])
            incoming[1], m, dq, na, ready = lax.optimization_barrier(
                (incoming[1], m, dq, na, ready)
            )
        mixed.append(m)
        d_query.append(dq)
        near.append(na)

    acc = add_rows(codes[0][None, :], back[0])
    low, high = beside(near[0][:2].astype(BF), near[-1][-2:].astype(BF))
    low, high, acc, back[1] = lax.optimization_barrier((low, high, acc, back[1]))
    sums = []
    for c, (first, count) in enumerate(PARTS):
        total = near[c][2 : 2 + count]
        prior = low.astype(F32) if c == 0 else near[c - 1][-2:]
        nextp = high.astype(F32) if c == len(PARTS) - 1 else near[c + 1][:2]
        rest = jnp.zeros((count - 4, BLOCK, 2 * D), F32)
        sums.append(total + jnp.concatenate([prior, rest, nextp], axis=0))
    near_sum = jnp.concatenate(sums, axis=0).astype(BF).reshape(BLK_DEV * BLOCK, 2 * D)
    d_q = jnp.concatenate(d_query, axis=0).reshape(BLK_DEV * BLOCK, D)
    base = dot(d_q, w_qt) + dot(near_sum, w_kvt)

    far_sum = last_add_rows(codes[1][None, :], back[1], acc)
    far = exchange(far_sum.reshape(NDEV, FOLD, WIDE)).reshape(NDEV * FOLD, WIDE)
    node_grad = finish(base.reshape(BLK_DEV, BLOCK, D), far)
    mixed = jnp.concatenate(mixed, axis=0).reshape(BLK_DEV * BLOCK, D)
    return mixed, node_grad.reshape(BLK_DEV * BLOCK, D)


def solution(mesh):
    rows = P(AXES, None)
    return jax.shard_map(
        on_device,
        mesh=mesh,
        in_specs=(rows, P(), P(), P(), P(), rows, P(), rows, rows),
        out_specs=(rows, rows),
        check_vma=False,
    )
```

```python
import jax
import jax.numpy as jnp
from jax import lax
from jax.experimental import pallas as pl
from jax.experimental.pallas import tpu as pltpu
from jax.sharding import PartitionSpec as P

HEADS = 8
HEAD = 64
BLOCK = 128
LOCD = 3
EXPD = 4
VIRT = 16
BLK_DEV = 12
D = 512
NB = 1536
NDEV = 128
FOLD = 8
WIDE = D + D // 2
HALF = D // 2
SPLIT = NDEV * FOLD
PARTS = ((0, 4), (4, 8))
NEAR = LOCD * BLOCK
LISTED = (LOCD + EXPD) * BLOCK
KEYS = LISTED + VIRT
AXES = ("group", "dev")
BF = jnp.bfloat16
F32 = jnp.float32
NT = (((1,), (1,)), ((), ()))
TN = (((0,), (0,)), ((), ()))


def dot(a, b, dims=None):
    if dims is None:
        return jnp.dot(a, b, preferred_element_type=F32)
    return lax.dot_general(a, b, dims, preferred_element_type=F32)


def params(mib):
    return pltpu.CompilerParams(vmem_limit_bytes=mib * 1024 * 1024)


def cost(flops, nbytes):
    return pl.CostEstimate(flops=flops, bytes_accessed=nbytes, transcendentals=0)


def swap_matrix():
    row = lax.broadcasted_iota(jnp.int32, (256, 256), 0)
    col = lax.broadcasted_iota(jnp.int32, (256, 256), 1)
    return jnp.where(col == (row % 16) * 16 + row // 16, 1.0, 0.0).astype(BF)


def fold_matrices(transposed):
    shape = (BLK_DEV * 16, 16 * FOLD) if transposed else (16 * FOLD, BLK_DEV * 16)
    folded = lax.broadcasted_iota(jnp.int32, shape, 1 if transposed else 0)
    plain = lax.broadcasted_iota(jnp.int32, shape, 0 if transposed else 1)
    same = folded // FOLD == plain % 16
    row, block = folded % FOLD, plain // 16
    return [
        jnp.where(same & hit, 1.0, 0.0).astype(BF)
        for hit in (block == row, (block == row + 8) & (row < 4), (block == row + 4) & (row >= 4))
    ]


def stripe_kernel(x_ref, out_ref):
    whole, left, right = fold_matrices(False)
    for g in range(x_ref.shape[1] // 16):
        rows = x_ref[:, 16 * g : 16 * g + 16, :].reshape(BLK_DEV * 16, D)
        part = slice(16 * FOLD * g, 16 * FOLD * (g + 1))
        out_ref[part, :D] = dot(whole, rows).astype(BF)
        out_ref[part, D:] = (dot(left, rows[:, :HALF]) + dot(right, rows[:, HALF:])).astype(BF)


def stripe(x):
    step = 64
    return pl.pallas_call(
        stripe_kernel,
        grid=(BLOCK // step,),
        in_specs=[pl.BlockSpec((BLK_DEV, step, D), lambda i: (0, i, 0))],
        out_specs=pl.BlockSpec((step * FOLD, WIDE), lambda i: (i, 0)),
        out_shape=jax.ShapeDtypeStruct((BLOCK * FOLD, WIDE), BF),
        compiler_params=params(58),
        name="stripe",
    )(x)


def project_kernel(x_ref, w_ref, kv_ref):
    kv_ref[...] = dot(x_ref[...].reshape(4 * BLOCK, D), w_ref[...]).astype(BF).reshape(4, BLOCK, 2 * D)


def project(x_ext, w_kv, first, count):
    return pl.pallas_call(
        project_kernel,
        grid=(count // 4,),
        in_specs=[
            pl.BlockSpec((4, BLOCK, D), lambda i: (first // 4 + i, 0, 0)),
            pl.BlockSpec((D, 2 * D), lambda i: (0, 0)),
        ],
        out_specs=pl.BlockSpec((4, BLOCK, 2 * D), lambda i: (i, 0, 0)),
        out_shape=jax.ShapeDtypeStruct((count, BLOCK, 2 * D), BF),
        compiler_params=params(20),
        cost_estimate=cost(count * 150_000_000, 12_000_000),
        name="project",
    )(x_ext, w_kv)


def sides_kernel(x_ref, grad_ref, wqt_ref, wo_ref, out_ref):
    out_ref[...] = jnp.zeros_like(out_ref)
    qt = (dot(wqt_ref[...], x_ref[...].reshape(-1, D), NT).astype(BF) * HEAD**-0.5).astype(BF)
    dat = dot(wo_ref[...], grad_ref[...].reshape(-1, D), NT).astype(BF)
    for i in range(x_ref.shape[0]):
        part = slice(i * BLOCK, (i + 1) * BLOCK)
        for h in range(HEADS):
            out_ref[i, h, :HEAD, :BLOCK] = qt[h * HEAD : (h + 1) * HEAD, part]
            out_ref[i, h, HEAD:, BLOCK:] = dat[h * HEAD : (h + 1) * HEAD, part]


def make_sides(x, grads, w_qt, wo, first, count):
    step = 4
    rows = pl.BlockSpec((step, BLOCK, D), lambda i: (first // step + i, 0, 0))
    weight = pl.BlockSpec((D, D), lambda i: (0, 0))
    return pl.pallas_call(
        sides_kernel,
        grid=(count // step,),
        in_specs=[rows, rows, weight, weight],
        out_specs=pl.BlockSpec((step, HEADS, BLOCK, 2 * BLOCK), lambda i: (i, 0, 0, 0)),
        out_shape=jax.ShapeDtypeStruct((count, HEADS, BLOCK, 2 * BLOCK), BF),
        compiler_params=params(20),
        cost_estimate=cost(count * 150_000_000, count * 800_000),
        name="make_sides",
    )(x, grads, w_qt, wo)


def unfold_matrices(transposed):
    shape = (SPLIT, SPLIT // 2) if transposed else (SPLIT // 2, SPLIT)
    folded = lax.broadcasted_iota(jnp.int32, shape, 0 if transposed else 1)
    plain = lax.broadcasted_iota(jnp.int32, shape, 1 if transposed else 0)
    left = plain // 4 * FOLD + plain % 4
    return [jnp.where(folded == left + shift, 1.0, 0.0).astype(BF) for shift in (0, 4)]


def spread_kernel(codes_ref, out_ref):
    for i in range(codes_ref.shape[0]):
        row = jnp.broadcast_to(codes_ref[i : i + 1, :], (BLOCK, BLOCK))
        out_ref[i * BLOCK : (i + 1) * BLOCK, :] = row.T


def spread(codes):
    n = codes.shape[0]
    return pl.pallas_call(
        spread_kernel,
        out_shape=jax.ShapeDtypeStruct((n, BLOCK), jnp.int32),
        compiler_params=params(8),
        name="spread",
    )(codes.reshape(n // BLOCK, BLOCK))


def pick_kernel(codes_ref, stripes_ref, out_ref, table):
    @pl.when(pl.program_id(0) == 0)
    def _():
        left, right = unfold_matrices(False)
        table[:SPLIT, :] = stripes_ref[:, :D]
        halves = stripes_ref[:, D:]
        table[SPLIT:, :HALF] = dot(left, halves).astype(BF)
        table[SPLIT:, HALF:] = dot(right, halves).astype(BF)

    codes = codes_ref[...]
    at = lax.broadcasted_iota(jnp.int32, codes.shape, 1)
    pick = [jnp.where(codes == at + k, 1.0, 0.0).astype(BF) for k in range(0, NB, BLOCK)]
    out_ref[...] = dot(jnp.concatenate(pick, axis=1), table[...]).astype(BF)


def pick_rows(codes, stripes):
    n = codes.shape[0]
    step = 1024
    return pl.pallas_call(
        pick_kernel,
        grid=(n // step,),
        in_specs=[
            pl.BlockSpec((step, BLOCK), lambda i: (i, 0)),
            pl.BlockSpec((SPLIT, WIDE), lambda i: (0, 0)),
        ],
        out_specs=pl.BlockSpec((step, D), lambda i: (i, 0)),
        out_shape=jax.ShapeDtypeStruct((n, D), BF),
        scratch_shapes=[pltpu.VMEM((NB, D), BF)],
        compiler_params=params(58),
        cost_estimate=cost(n * 2_100_000, 6_000_000),
        name="pick_rows",
    )(codes, stripes)


def add_kernel(codes_ref, rows_ref, out_ref):
    step, n = out_ref.shape[0], rows_ref.shape[0]
    at = lax.broadcasted_iota(jnp.int32, (step, n), 0) + pl.program_id(0) * step
    pick = jnp.where(codes_ref[...] == at, 1.0, 0.0).astype(BF)
    out_ref[...] = dot(pick, rows_ref[...])


def add_rows(codes, rows):
    n = rows.shape[0]
    step = 512
    return pl.pallas_call(
        add_kernel,
        grid=(NB // step,),
        in_specs=[
            pl.BlockSpec((1, n), lambda i: (0, 0)),
            pl.BlockSpec((n, D), lambda i: (0, 0)),
        ],
        out_specs=pl.BlockSpec((step, D), lambda i: (i, 0)),
        out_shape=jax.ShapeDtypeStruct((NB, D), F32),
        compiler_params=params(40),
        cost_estimate=cost(n * 1_600_000, 8_000_000),
        name="add_rows",
    )(codes, rows)


def last_add_kernel(codes_ref, rows_ref, acc_ref, out_ref):
    step, n = acc_ref.shape[0], rows_ref.shape[0]
    at = lax.broadcasted_iota(jnp.int32, (step, n), 0) + pl.program_id(0) * step
    pick = jnp.where(codes_ref[...] == at, 1.0, 0.0).astype(BF)
    total = (acc_ref[...] + dot(pick, rows_ref[...])).astype(BF)
    for i in range(SPLIT // step):

        @pl.when(pl.program_id(0) == i)
        def _():
            out_ref[i * step : (i + 1) * step, :D] = total

    @pl.when(pl.program_id(0) == SPLIT // step)
    def _():
        left, right = unfold_matrices(True)
        out_ref[:, D:] = (dot(left, total[:, :HALF]) + dot(right, total[:, HALF:])).astype(BF)


def last_add_rows(codes, rows, acc):
    n = rows.shape[0]
    step = SPLIT // 2
    return pl.pallas_call(
        last_add_kernel,
        grid=(NB // step,),
        in_specs=[
            pl.BlockSpec((1, n), lambda i: (0, 0)),
            pl.BlockSpec((n, D), lambda i: (0, 0)),
            pl.BlockSpec((step, D), lambda i: (i, 0)),
        ],
        out_specs=pl.BlockSpec((SPLIT, WIDE), lambda i: (0, 0)),
        out_shape=jax.ShapeDtypeStruct((SPLIT, WIDE), BF),
        compiler_params=params(58),
        cost_estimate=cost(n * 1_600_000, 8_000_000),
        name="last_add_rows",
    )(codes, rows, acc)


def finish_kernel(base_ref, far_ref, out_ref):
    whole, left, right = fold_matrices(True)
    for g in range(base_ref.shape[1] // 16):
        part = slice(16 * g, 16 * g + 16)
        rows = far_ref[16 * FOLD * g : 16 * FOLD * (g + 1)]
        main = dot(whole, rows[:, :D])
        halves = rows[:, D:]
        low = (main[:, :HALF] + dot(left, halves)).reshape(BLK_DEV, 16, HALF)
        high = (main[:, HALF:] + dot(right, halves)).reshape(BLK_DEV, 16, HALF)
        out_ref[:, part, :HALF] = (base_ref[:, part, :HALF] + low).astype(BF)
        out_ref[:, part, HALF:] = (base_ref[:, part, HALF:] + high).astype(BF)


def finish(base, far):
    step = 32
    rows = pl.BlockSpec((BLK_DEV, step, D), lambda i: (0, i, 0))
    return pl.pallas_call(
        finish_kernel,
        grid=(BLOCK // step,),
        in_specs=[rows, pl.BlockSpec((step * FOLD, WIDE), lambda i: (i, 0))],
        out_specs=rows,
        out_shape=jax.ShapeDtypeStruct((BLK_DEV, BLOCK, D), BF),
        compiler_params=params(16),
        name="finish",
    )(base, far)


def scaled(side, inverse):
    both = jnp.concatenate([inverse, inverse], axis=1)
    return (side.astype(F32) * both).astype(BF)


def head_cols(h):
    return slice(h * 2 * HEAD, (h + 1) * 2 * HEAD)


def far_kernel(
    rel_ref,
    live_ref,
    sides_ref,
    kvx_ref,
    far_ref,
    vkv_ref,
    wkv_ref,
    wkvt_ref,
    back_ref,
    pairs_ref,
    kv_ref,
    inverse_ref,
    far_rows,
    far_grads,
    bias,
    ones,
    scores,
    d_probs,
    tops,
):
    b = pl.program_id(0)
    kv = kv_ref.at[0]

    @pl.when(b == 0)
    def _():
        bias[LISTED:KEYS, :] = jnp.zeros((VIRT, BLOCK), BF)
        lane = lax.broadcasted_iota(jnp.int32, (BLOCK, 2 * BLOCK), 1)
        row = lax.broadcasted_iota(jnp.int32, (BLOCK, 2 * BLOCK), 0)
        ones[...] = jnp.where((row == 0) & (lane < BLOCK), 1.0, 0.0).astype(BF)

    turn = lax.rem(b, 4)

    @pl.when(turn == 0)
    def _():
        swap = swap_matrix()
        for g in range(0, BLOCK, 16):
            rows = dot(swap, far_ref[g : g + 16].reshape(256, D)).astype(BF)
            far_rows[:, g : g + 16, :] = rows.reshape(16, 16, D)

    far_x = far_rows[pl.ds(turn * EXPD, EXPD)].reshape(EXPD * BLOCK, D)
    kv[NEAR:LISTED, :] = dot(far_x, wkv_ref[...]).astype(BF)
    kv[LISTED:KEYS, :] = vkv_ref[...]
    for s in range(LOCD):
        kv[s * BLOCK : (s + 1) * BLOCK, :] = kvx_ref[rel_ref[b, s]]
    key = lax.broadcasted_iota(jnp.int32, (BLOCK, BLOCK), 0)
    lane = lax.broadcasted_iota(jnp.int32, (BLOCK, BLOCK), 1)
    for s in range(LOCD + EXPD):
        part = slice(s * BLOCK, (s + 1) * BLOCK)
        closed = (key >= live_ref[b, s]) & (lane == 0)
        bias[part, :] = jnp.where(closed, -1e30, 0.0).astype(BF)

    def products(h):
        if h < HEADS:
            side = jnp.concatenate([sides_ref[0, h], ones[...]], axis=0)
            top = None
            for part in (slice(0, 464), slice(464, KEYS)):
                keys = jnp.concatenate([kv[part, head_cols(h)], bias[part, :]], axis=1)
                both = dot(keys, side)
                scores[h % 2, part, :] = both[:, :BLOCK]
                d_probs[h % 2, part, :] = both[:, BLOCK:].astype(BF)
                most = jnp.max(both[:, :BLOCK].reshape(-1, 8, BLOCK), axis=0)
                top = most if top is None else jnp.maximum(top, most)
                yield
            tops[h % 2] = top
        g = h - 2
        if g >= 0:
            inverse = inverse_ref[0, g : g + 1, :]
            side = scaled(sides_ref[0, g], inverse)
            far_grads[:, head_cols(g)] = dot(pairs_ref[0, g, NEAR:LISTED, :], side, NT).astype(BF)
            yield

    def soften(h):
        if h < 0 or h >= HEADS:
            return
        now, d_now = scores.at[h % 2], d_probs.at[h % 2]
        pair = pairs_ref.at[0, h]
        step = 48
        folded = (step // 8, 8, BLOCK)
        parts = [slice(r, r + step) for r in range(0, KEYS, step)]
        top = jnp.max(tops[h % 2], axis=0, keepdims=True)
        total = jnp.zeros((8, BLOCK), F32)
        drift = jnp.zeros((8, BLOCK), F32)
        for part in parts:
            weights = jnp.exp(now[part, :] - top)
            total += jnp.sum(weights.reshape(folded), axis=0)
            weights = weights.astype(BF)
            pair[part, BLOCK:] = weights
            moved = (weights * d_now[part, :]).astype(F32)
            drift += jnp.sum(moved.reshape(folded), axis=0)
            yield
        inverse = 1.0 / jnp.sum(total, axis=0, keepdims=True)
        inverse_ref[0, h : h + 1, :] = inverse
        delta = (jnp.sum(drift, axis=0, keepdims=True) * inverse).astype(BF)
        for part in parts:
            pair[part, :BLOCK] = pair[part, BLOCK:] * (d_now[part, :] - delta)
            yield

    done = object()
    for h in range(HEADS + 2):
        vector, matrix = soften(h - 1), products(h)
        running = True
        while running:
            running = next(matrix, done) is not done
            for _ in range(16):
                running = next(vector, done) is not done or running

    far_term = dot(far_grads[...], wkvt_ref[...]).astype(BF)
    far_rows[pl.ds(turn * EXPD, EXPD)] = far_term.reshape(EXPD, BLOCK, D)

    @pl.when(turn == 3)
    def _():
        swap = swap_matrix()
        for g in range(0, BLOCK, 16):
            rows = far_rows[:, g : g + 16, :].reshape(256, D)
            back_ref[g : g + 16] = dot(swap, rows).astype(BF).reshape(16, 16, D)


def whole(*shape):
    return pl.BlockSpec(shape, lambda b: (0,) * len(shape), pipeline_mode=pl.Buffered(1))


def kept(*shape):
    return pl.BlockSpec(shape, lambda b: (0,) * len(shape))


def of_query(first, *shape):
    return pl.BlockSpec((1,) + shape, lambda b: (first + b,) + (0,) * len(shape))


def far_part(rel, live, sides, kvx, far, vkv, wkv, wkvt):
    count = rel.shape[0]
    listed = count * EXPD
    fours = pl.BlockSpec((BLOCK, 16, D), lambda b: (0, b // 4, 0))
    smem = pl.BlockSpec(memory_space=pltpu.SMEM)
    return pl.pallas_call(
        far_kernel,
        grid=(count,),
        in_specs=[
            smem,
            smem,
            of_query(0, HEADS, BLOCK, 2 * BLOCK),
            whole(count + 4, BLOCK, 2 * D),
            fours,
            whole(VIRT, 2 * D),
            whole(D, 2 * D),
            whole(2 * D, D),
        ],
        out_specs=[
            fours,
            of_query(0, HEADS, KEYS, 2 * BLOCK),
            of_query(0, KEYS, 2 * D),
            of_query(0, HEADS, BLOCK),
        ],
        out_shape=[
            jax.ShapeDtypeStruct((BLOCK, listed, D), BF),
            jax.ShapeDtypeStruct((count, HEADS, KEYS, 2 * BLOCK), BF),
            jax.ShapeDtypeStruct((count, KEYS, 2 * D), BF),
            jax.ShapeDtypeStruct((count, HEADS, BLOCK), F32),
        ],
        scratch_shapes=[
            pltpu.VMEM((16, BLOCK, D), BF),
            pltpu.VMEM((EXPD * BLOCK, 2 * D), BF),
            pltpu.VMEM((KEYS, BLOCK), BF),
            pltpu.VMEM((BLOCK, 2 * BLOCK), BF),
            pltpu.VMEM((2, KEYS, BLOCK), F32),
            pltpu.VMEM((2, KEYS, BLOCK), BF),
            pltpu.VMEM((2, 8, BLOCK), F32),
        ],
        compiler_params=params(46),
        cost_estimate=cost(count * 6_500_000_000, count * 7_000_000),
        name="far_part",
    )(rel, live, sides, kvx, far, vkv, wkv, wkvt)


def near_kernel(
    rel_ref, sides_ref, pairs_ref, kv_ref, inverse_ref, wo_ref, mixed_ref, dq_ref, near_ref, near_grads, att, dqt
):
    b = pl.program_id(0)

    @pl.when(b == 0)
    def _():
        near_ref[...] = jnp.zeros_like(near_ref)

    for h in range(HEADS):
        rows = slice(h * HEAD, (h + 1) * HEAD)
        sums = dot(kv_ref[0, :, head_cols(h)], pairs_ref[0, h], TN)
        inverse = inverse_ref[0, h : h + 1, :]
        dqt[rows, :] = sums[:HEAD, :BLOCK] * inverse
        att[rows, :] = sums[HEAD:, BLOCK:] * inverse
        side = scaled(sides_ref[0, h], inverse)
        near_grads[:, head_cols(h)] = dot(pairs_ref[0, h, :NEAR, :], side, NT)
    for s in range(LOCD):
        near_ref[rel_ref[b, s]] += near_grads[s * BLOCK : (s + 1) * BLOCK, :]
    mixed_ref[0] = dot(att[...].T.astype(BF), wo_ref[...]).astype(BF)
    dq_ref[0] = (dqt[...] * HEAD**-0.5).T.astype(BF)


def near_part(rel, sides, pairs, kv, inverse, wo):
    count = rel.shape[0]
    return pl.pallas_call(
        near_kernel,
        grid=(count,),
        in_specs=[
            pl.BlockSpec(memory_space=pltpu.SMEM),
            of_query(0, HEADS, BLOCK, 2 * BLOCK),
            of_query(0, HEADS, KEYS, 2 * BLOCK),
            of_query(0, KEYS, 2 * D),
            of_query(0, HEADS, BLOCK),
            whole(D, D),
        ],
        out_specs=[
            of_query(0, BLOCK, D),
            of_query(0, BLOCK, D),
            kept(count + 4, BLOCK, 2 * D),
        ],
        out_shape=[
            jax.ShapeDtypeStruct((count, BLOCK, D), BF),
            jax.ShapeDtypeStruct((count, BLOCK, D), BF),
            jax.ShapeDtypeStruct((count + 4, BLOCK, 2 * D), F32),
        ],
        scratch_shapes=[
            pltpu.VMEM((NEAR, 2 * D), F32),
            pltpu.VMEM((D, BLOCK), F32),
            pltpu.VMEM((D, BLOCK), F32),
        ],
        compiler_params=params(34),
        cost_estimate=cost(count * 3_500_000_000, count * 7_000_000),
        name="near_part",
    )(rel, sides, pairs, kv, inverse, wo)


def exchange(rows):
    return lax.all_to_all(rows, AXES, split_axis=0, concat_axis=0, tiled=True)


def beside(low, high):
    up = [(i, i + 1) for i in range(NDEV - 1)]
    down = [(j, i) for i, j in up]
    return lax.ppermute(high, AXES, up), lax.ppermute(low, AXES, down)


def on_device(
    node_features,
    virtual_features,
    w_qkv,
    output_weight,
    block_home,
    local_blocks,
    expander_blocks,
    key_live,
    out_grad,
):
    me = lax.axis_index(AXES)
    x = node_features.reshape(BLK_DEV, BLOCK, D)
    grads = out_grad.reshape(BLK_DEV, BLOCK, D)
    striped = stripe(x)
    stripes = exchange(striped.reshape(NDEV, FOLD, WIDE)).reshape(NDEV * FOLD, WIDE)

    w_kv = w_qkv[:, D:].reshape(D, 2, HEADS, HEAD).transpose(0, 2, 1, 3).reshape(D, 2 * D)

    graph = jnp.arange(NB, dtype=jnp.int32)

    def stored_at(ids, home):
        same = ids[..., None] == graph
        return jnp.sum(jnp.where(same, home, 0), axis=-1, dtype=jnp.int32)

    near_at = stored_at(local_blocks, block_home)
    rel = near_at - (me * BLK_DEV - 2)
    owner, inner = block_home // BLK_DEV, block_home % BLK_DEV
    code = jnp.where(inner < FOLD, owner * FOLD + inner, SPLIT + owner * 4 + inner - FOLD)
    far_codes = stored_at(expander_blocks.reshape(NDEV, BLK_DEV * EXPD), code)
    low_x, high_x, far_codes = lax.optimization_barrier((x[:2], x[BLK_DEV - 2 :], far_codes))
    before, after = beside(low_x, high_x)
    codes = [far_codes[:, EXPD * f : EXPD * (f + n)].reshape(-1) for f, n in PARTS]
    tall = spread(codes[0])
    stripes, before, after, w_kv, rel, tall, codes = lax.optimization_barrier(
        (stripes, before, after, w_kv, rel, tall, codes)
    )
    w_kvt = w_kv.T
    w_qt = w_qkv[:, :D].T
    vkv = dot(virtual_features, w_kv).astype(BF)

    rows = pick_rows(tall, stripes)
    incoming = exchange(rows.reshape(NDEV, -1, D))
    later = pick_rows(spread(codes[1]), stripes)
    x_ext = jnp.concatenate([before, x, after], axis=0)

    def prepared(first, count):
        kvx = project(x_ext, w_kv, first, count + 4)
        return kvx, make_sides(x, grads, w_qt, output_weight, first, count)

    ready = prepared(*PARTS[0])
    incoming, later, ready, x_ext = lax.optimization_barrier((incoming, later, ready, x_ext))
    incoming = [incoming, exchange(later.reshape(NDEV, -1, D))]

    mixed, d_query, near, back = [], [], [], []
    for c, (first, count) in enumerate(PARTS):
        own = rel[first : first + count] - first
        live = key_live[first : first + count]
        kvx, sides = ready
        far_back, pairs, kv, inverse = far_part(
            own, live, sides, kvx, incoming[c], vkv, w_kv, w_kvt
        )
        back.append(exchange(far_back).reshape(-1, D))
        m, dq, na = near_part(own, sides, pairs, kv, inverse, output_weight)
        if c == 0:
            ready = prepared(*PARTS[1])
            incoming[1], m, dq, na, ready = lax.optimization_barrier(
                (incoming[1], m, dq, na, ready)
            )
        mixed.append(m)
        d_query.append(dq)
        near.append(na)

    acc = add_rows(codes[0][None, :], back[0])
    low, high = beside(near[0][:2].astype(BF), near[-1][-2:].astype(BF))
    low, high, acc, back[1] = lax.optimization_barrier((low, high, acc, back[1]))
    sums = []
    for c, (first, count) in enumerate(PARTS):
        total = near[c][2 : 2 + count]
        prior = low.astype(F32) if c == 0 else near[c - 1][-2:]
        nextp = high.astype(F32) if c == len(PARTS) - 1 else near[c + 1][:2]
        rest = jnp.zeros((count - 4, BLOCK, 2 * D), F32)
        sums.append(total + jnp.concatenate([prior, rest, nextp], axis=0))
    near_sum = jnp.concatenate(sums, axis=0).astype(BF).reshape(BLK_DEV * BLOCK, 2 * D)
    d_q = jnp.concatenate(d_query, axis=0).reshape(BLK_DEV * BLOCK, D)
    base = dot(d_q, w_qt) + dot(near_sum, w_kvt)

    far_sum = last_add_rows(codes[1][None, :], back[1], acc)
    far = exchange(far_sum.reshape(NDEV, FOLD, WIDE)).reshape(NDEV * FOLD, WIDE)
    node_grad = finish(base.reshape(BLK_DEV, BLOCK, D), far)
    mixed = jnp.concatenate(mixed, axis=0).reshape(BLK_DEV * BLOCK, D)
    return mixed, node_grad.reshape(BLK_DEV * BLOCK, D)


def solution(mesh):
    rows = P(AXES, None)
    return jax.shard_map(
        on_device,
        mesh=mesh,
        in_specs=(rows, P(), P(), P(), P(), rows, P(), rows, rows),
        out_specs=(rows, rows),
        check_vma=False,
    )
```

```python
import jax
import jax.numpy as jnp
from jax import lax
from jax.experimental import pallas as pl
from jax.experimental.pallas import tpu as pltpu
from jax.sharding import PartitionSpec as P

HEADS = 8
HEAD = 64
BLOCK = 128
LOCD = 3
EXPD = 4
VIRT = 16
BLK_DEV = 12
D = 512
NB = 1536
NDEV = 128
FOLD = 8
WIDE = D + D // 2
HALF = D // 2
SPLIT = NDEV * FOLD
PARTS = ((0, 4), (4, 8))
NEAR = LOCD * BLOCK
LISTED = (LOCD + EXPD) * BLOCK
KEYS = LISTED + VIRT
AXES = ("group", "dev")
BF = jnp.bfloat16
F32 = jnp.float32
NT = (((1,), (1,)), ((), ()))
TN = (((0,), (0,)), ((), ()))


def dot(a, b, dims=None):
    if dims is None:
        return jnp.dot(a, b, preferred_element_type=F32)
    return lax.dot_general(a, b, dims, preferred_element_type=F32)


def params(mib):
    return pltpu.CompilerParams(vmem_limit_bytes=mib * 1024 * 1024)


def cost(flops, nbytes):
    return pl.CostEstimate(flops=flops, bytes_accessed=nbytes, transcendentals=0)


def swap_matrix():
    row = lax.broadcasted_iota(jnp.int32, (256, 256), 0)
    col = lax.broadcasted_iota(jnp.int32, (256, 256), 1)
    return jnp.where(col == (row % 16) * 16 + row // 16, 1.0, 0.0).astype(BF)


def fold_matrices(transposed):
    shape = (BLK_DEV * 16, 16 * FOLD) if transposed else (16 * FOLD, BLK_DEV * 16)
    folded = lax.broadcasted_iota(jnp.int32, shape, 1 if transposed else 0)
    plain = lax.broadcasted_iota(jnp.int32, shape, 0 if transposed else 1)
    same = folded // FOLD == plain % 16
    row, block = folded % FOLD, plain // 16
    return [
        jnp.where(same & hit, 1.0, 0.0).astype(BF)
        for hit in (block == row, (block == row + 8) & (row < 4), (block == row + 4) & (row >= 4))
    ]


def stripe_kernel(x_ref, out_ref):
    whole, left, right = fold_matrices(False)
    for g in range(x_ref.shape[1] // 16):
        rows = x_ref[:, 16 * g : 16 * g + 16, :].reshape(BLK_DEV * 16, D)
        part = slice(16 * FOLD * g, 16 * FOLD * (g + 1))
        out_ref[part, :D] = dot(whole, rows).astype(BF)
        out_ref[part, D:] = (dot(left, rows[:, :HALF]) + dot(right, rows[:, HALF:])).astype(BF)


def stripe(x):
    step = 64
    return pl.pallas_call(
        stripe_kernel,
        grid=(BLOCK // step,),
        in_specs=[pl.BlockSpec((BLK_DEV, step, D), lambda i: (0, i, 0))],
        out_specs=pl.BlockSpec((step * FOLD, WIDE), lambda i: (i, 0)),
        out_shape=jax.ShapeDtypeStruct((BLOCK * FOLD, WIDE), BF),
        compiler_params=params(58),
        name="stripe",
    )(x)


def project_kernel(x_ref, w_ref, kv_ref):
    kv_ref[...] = dot(x_ref[...].reshape(4 * BLOCK, D), w_ref[...]).astype(BF).reshape(4, BLOCK, 2 * D)


def project(x_ext, w_kv, first, count):
    return pl.pallas_call(
        project_kernel,
        grid=(count // 4,),
        in_specs=[
            pl.BlockSpec((4, BLOCK, D), lambda i: (first // 4 + i, 0, 0)),
            pl.BlockSpec((D, 2 * D), lambda i: (0, 0)),
        ],
        out_specs=pl.BlockSpec((4, BLOCK, 2 * D), lambda i: (i, 0, 0)),
        out_shape=jax.ShapeDtypeStruct((count, BLOCK, 2 * D), BF),
        compiler_params=params(20),
        cost_estimate=cost(count * 150_000_000, 12_000_000),
        name="project",
    )(x_ext, w_kv)


def sides_kernel(x_ref, grad_ref, wqt_ref, wo_ref, out_ref):
    out_ref[...] = jnp.zeros_like(out_ref)
    qt = (dot(wqt_ref[...], x_ref[...].reshape(-1, D), NT).astype(BF) * HEAD**-0.5).astype(BF)
    dat = dot(wo_ref[...], grad_ref[...].reshape(-1, D), NT).astype(BF)
    for i in range(x_ref.shape[0]):
        part = slice(i * BLOCK, (i + 1) * BLOCK)
        for h in range(HEADS):
            out_ref[i, h, :HEAD, :BLOCK] = qt[h * HEAD : (h + 1) * HEAD, part]
            out_ref[i, h, HEAD:, BLOCK:] = dat[h * HEAD : (h + 1) * HEAD, part]


def make_sides(x, grads, w_qt, wo, first, count):
    step = 4
    rows = pl.BlockSpec((step, BLOCK, D), lambda i: (first // step + i, 0, 0))
    weight = pl.BlockSpec((D, D), lambda i: (0, 0))
    return pl.pallas_call(
        sides_kernel,
        grid=(count // step,),
        in_specs=[rows, rows, weight, weight],
        out_specs=pl.BlockSpec((step, HEADS, BLOCK, 2 * BLOCK), lambda i: (i, 0, 0, 0)),
        out_shape=jax.ShapeDtypeStruct((count, HEADS, BLOCK, 2 * BLOCK), BF),
        compiler_params=params(20),
        cost_estimate=cost(count * 150_000_000, count * 800_000),
        name="make_sides",
    )(x, grads, w_qt, wo)


def unfold_matrices(transposed):
    shape = (SPLIT, SPLIT // 2) if transposed else (SPLIT // 2, SPLIT)
    folded = lax.broadcasted_iota(jnp.int32, shape, 0 if transposed else 1)
    plain = lax.broadcasted_iota(jnp.int32, shape, 1 if transposed else 0)
    left = plain // 4 * FOLD + plain % 4
    return [jnp.where(folded == left + shift, 1.0, 0.0).astype(BF) for shift in (0, 4)]


def spread_kernel(codes_ref, out_ref):
    for i in range(codes_ref.shape[0]):
        row = jnp.broadcast_to(codes_ref[i : i + 1, :], (BLOCK, BLOCK))
        out_ref[i * BLOCK : (i + 1) * BLOCK, :] = row.T


def spread(codes):
    n = codes.shape[0]
    return pl.pallas_call(
        spread_kernel,
        out_shape=jax.ShapeDtypeStruct((n, BLOCK), jnp.int32),
        compiler_params=params(8),
        name="spread",
    )(codes.reshape(n // BLOCK, BLOCK))


def pick_kernel(codes_ref, stripes_ref, out_ref, table):
    @pl.when(pl.program_id(0) == 0)
    def _():
        left, right = unfold_matrices(False)
        table[:SPLIT, :] = stripes_ref[:, :D]
        halves = stripes_ref[:, D:]
        table[SPLIT:, :HALF] = dot(left, halves).astype(BF)
        table[SPLIT:, HALF:] = dot(right, halves).astype(BF)

    codes = codes_ref[...]
    at = lax.broadcasted_iota(jnp.int32, codes.shape, 1)
    pick = [jnp.where(codes == at + k, 1.0, 0.0).astype(BF) for k in range(0, NB, BLOCK)]
    out_ref[...] = dot(jnp.concatenate(pick, axis=1), table[...]).astype(BF)


def pick_rows(codes, stripes):
    n = codes.shape[0]
    step = 512
    return pl.pallas_call(
        pick_kernel,
        grid=(n // step,),
        in_specs=[
            pl.BlockSpec((step, BLOCK), lambda i: (i, 0)),
            pl.BlockSpec((SPLIT, WIDE), lambda i: (0, 0)),
        ],
        out_specs=pl.BlockSpec((step, D), lambda i: (i, 0)),
        out_shape=jax.ShapeDtypeStruct((n, D), BF),
        scratch_shapes=[pltpu.VMEM((NB, D), BF)],
        compiler_params=params(58),
        cost_estimate=cost(n * 2_100_000, 6_000_000),
        name="pick_rows",
    )(codes, stripes)


def add_kernel(codes_ref, rows_ref, out_ref):
    step, n = out_ref.shape[0], rows_ref.shape[0]
    at = lax.broadcasted_iota(jnp.int32, (step, n), 0) + pl.program_id(0) * step
    pick = jnp.where(codes_ref[...] == at, 1.0, 0.0).astype(BF)
    out_ref[...] = dot(pick, rows_ref[...])


def add_rows(codes, rows):
    n = rows.shape[0]
    step = 512
    return pl.pallas_call(
        add_kernel,
        grid=(NB // step,),
        in_specs=[
            pl.BlockSpec((1, n), lambda i: (0, 0)),
            pl.BlockSpec((n, D), lambda i: (0, 0)),
        ],
        out_specs=pl.BlockSpec((step, D), lambda i: (i, 0)),
        out_shape=jax.ShapeDtypeStruct((NB, D), F32),
        compiler_params=params(40),
        cost_estimate=cost(n * 1_600_000, 8_000_000),
        name="add_rows",
    )(codes, rows)


def last_add_kernel(codes_ref, rows_ref, acc_ref, out_ref):
    step, n = acc_ref.shape[0], rows_ref.shape[0]
    at = lax.broadcasted_iota(jnp.int32, (step, n), 0) + pl.program_id(0) * step
    pick = jnp.where(codes_ref[...] == at, 1.0, 0.0).astype(BF)
    total = (acc_ref[...] + dot(pick, rows_ref[...])).astype(BF)
    for i in range(SPLIT // step):

        @pl.when(pl.program_id(0) == i)
        def _():
            out_ref[i * step : (i + 1) * step, :D] = total

    @pl.when(pl.program_id(0) == SPLIT // step)
    def _():
        left, right = unfold_matrices(True)
        out_ref[:, D:] = (dot(left, total[:, :HALF]) + dot(right, total[:, HALF:])).astype(BF)


def last_add_rows(codes, rows, acc):
    n = rows.shape[0]
    step = SPLIT // 2
    return pl.pallas_call(
        last_add_kernel,
        grid=(NB // step,),
        in_specs=[
            pl.BlockSpec((1, n), lambda i: (0, 0)),
            pl.BlockSpec((n, D), lambda i: (0, 0)),
            pl.BlockSpec((step, D), lambda i: (i, 0)),
        ],
        out_specs=pl.BlockSpec((SPLIT, WIDE), lambda i: (0, 0)),
        out_shape=jax.ShapeDtypeStruct((SPLIT, WIDE), BF),
        compiler_params=params(58),
        cost_estimate=cost(n * 1_600_000, 8_000_000),
        name="last_add_rows",
    )(codes, rows, acc)


def finish_kernel(base_ref, far_ref, out_ref):
    whole, left, right = fold_matrices(True)
    for g in range(base_ref.shape[1] // 16):
        part = slice(16 * g, 16 * g + 16)
        rows = far_ref[16 * FOLD * g : 16 * FOLD * (g + 1)]
        main = dot(whole, rows[:, :D])
        halves = rows[:, D:]
        low = (main[:, :HALF] + dot(left, halves)).reshape(BLK_DEV, 16, HALF)
        high = (main[:, HALF:] + dot(right, halves)).reshape(BLK_DEV, 16, HALF)
        out_ref[:, part, :HALF] = (base_ref[:, part, :HALF] + low).astype(BF)
        out_ref[:, part, HALF:] = (base_ref[:, part, HALF:] + high).astype(BF)


def finish(base, far):
    step = 64
    rows = pl.BlockSpec((BLK_DEV, step, D), lambda i: (0, i, 0))
    return pl.pallas_call(
        finish_kernel,
        grid=(BLOCK // step,),
        in_specs=[rows, pl.BlockSpec((step * FOLD, WIDE), lambda i: (i, 0))],
        out_specs=rows,
        out_shape=jax.ShapeDtypeStruct((BLK_DEV, BLOCK, D), BF),
        compiler_params=params(16),
        name="finish",
    )(base, far)


def scaled(side, inverse):
    both = jnp.concatenate([inverse, inverse], axis=1)
    return (side.astype(F32) * both).astype(BF)


def head_cols(h):
    return slice(h * 2 * HEAD, (h + 1) * 2 * HEAD)


def far_kernel(
    rel_ref,
    live_ref,
    sides_ref,
    kvx_ref,
    far_ref,
    vkv_ref,
    wkv_ref,
    wkvt_ref,
    back_ref,
    pairs_ref,
    kv_ref,
    inverse_ref,
    far_rows,
    far_grads,
    bias,
    ones,
    scores,
    d_probs,
    tops,
):
    b = pl.program_id(0)
    kv = kv_ref.at[0]

    @pl.when(b == 0)
    def _():
        bias[LISTED:KEYS, :] = jnp.zeros((VIRT, BLOCK), BF)
        lane = lax.broadcasted_iota(jnp.int32, (BLOCK, 2 * BLOCK), 1)
        row = lax.broadcasted_iota(jnp.int32, (BLOCK, 2 * BLOCK), 0)
        ones[...] = jnp.where((row == 0) & (lane < BLOCK), 1.0, 0.0).astype(BF)

    turn = lax.rem(b, 4)

    @pl.when(turn == 0)
    def _():
        swap = swap_matrix()
        for g in range(0, BLOCK, 16):
            rows = dot(swap, far_ref[g : g + 16].reshape(256, D)).astype(BF)
            far_rows[:, g : g + 16, :] = rows.reshape(16, 16, D)

    far_x = far_rows[pl.ds(turn * EXPD, EXPD)].reshape(EXPD * BLOCK, D)
    kv[NEAR:LISTED, :] = dot(far_x, wkv_ref[...]).astype(BF)
    kv[LISTED:KEYS, :] = vkv_ref[...]
    for s in range(LOCD):
        kv[s * BLOCK : (s + 1) * BLOCK, :] = kvx_ref[rel_ref[b, s]]
    key = lax.broadcasted_iota(jnp.int32, (BLOCK, BLOCK), 0)
    lane = lax.broadcasted_iota(jnp.int32, (BLOCK, BLOCK), 1)
    for s in range(LOCD + EXPD):
        part = slice(s * BLOCK, (s + 1) * BLOCK)
        closed = (key >= live_ref[b, s]) & (lane == 0)
        bias[part, :] = jnp.where(closed, -1e30, 0.0).astype(BF)

    def products(h):
        if h < HEADS:
            side = jnp.concatenate([sides_ref[0, h], ones[...]], axis=0)
            top = None
            for part in (slice(0, 464), slice(464, KEYS)):
                keys = jnp.concatenate([kv[part, head_cols(h)], bias[part, :]], axis=1)
                both = dot(keys, side)
                scores[h % 2, part, :] = both[:, :BLOCK]
                d_probs[h % 2, part, :] = both[:, BLOCK:].astype(BF)
                most = jnp.max(both[:, :BLOCK].reshape(-1, 8, BLOCK), axis=0)
                top = most if top is None else jnp.maximum(top, most)
                yield
            tops[h % 2] = top
        g = h - 2
        if g >= 0:
            inverse = inverse_ref[0, g : g + 1, :]
            side = scaled(sides_ref[0, g], inverse)
            far_grads[:, head_cols(g)] = dot(pairs_ref[0, g, NEAR:LISTED, :], side, NT).astype(BF)
            yield

    def soften(h):
        if h < 0 or h >= HEADS:
            return
        now, d_now = scores.at[h % 2], d_probs.at[h % 2]
        pair = pairs_ref.at[0, h]
        step = 48
        folded = (step // 8, 8, BLOCK)
        parts = [slice(r, r + step) for r in range(0, KEYS, step)]
        top = jnp.max(tops[h % 2], axis=0, keepdims=True)
        total = jnp.zeros((8, BLOCK), F32)
        drift = jnp.zeros((8, BLOCK), F32)
        for part in parts:
            weights = jnp.exp(now[part, :] - top)
            total += jnp.sum(weights.reshape(folded), axis=0)
            weights = weights.astype(BF)
            pair[part, BLOCK:] = weights
            moved = (weights * d_now[part, :]).astype(F32)
            drift += jnp.sum(moved.reshape(folded), axis=0)
            yield
        inverse = 1.0 / jnp.sum(total, axis=0, keepdims=True)
        inverse_ref[0, h : h + 1, :] = inverse
        delta = (jnp.sum(drift, axis=0, keepdims=True) * inverse).astype(BF)
        for part in parts:
            pair[part, :BLOCK] = pair[part, BLOCK:] * (d_now[part, :] - delta)
            yield

    done = object()
    for h in range(HEADS + 2):
        vector, matrix = soften(h - 1), products(h)
        running = True
        while running:
            running = next(matrix, done) is not done
            for _ in range(16):
                running = next(vector, done) is not done or running

    far_term = dot(far_grads[...], wkvt_ref[...]).astype(BF)
    far_rows[pl.ds(turn * EXPD, EXPD)] = far_term.reshape(EXPD, BLOCK, D)

    @pl.when(turn == 3)
    def _():
        swap = swap_matrix()
        for g in range(0, BLOCK, 16):
            rows = far_rows[:, g : g + 16, :].reshape(256, D)
            back_ref[g : g + 16] = dot(swap, rows).astype(BF).reshape(16, 16, D)


def whole(*shape):
    return pl.BlockSpec(shape, lambda b: (0,) * len(shape), pipeline_mode=pl.Buffered(1))


def kept(*shape):
    return pl.BlockSpec(shape, lambda b: (0,) * len(shape))


def of_query(first, *shape):
    return pl.BlockSpec((1,) + shape, lambda b: (first + b,) + (0,) * len(shape))


def far_part(rel, live, sides, kvx, far, vkv, wkv, wkvt):
    count = rel.shape[0]
    listed = count * EXPD
    fours = pl.BlockSpec((BLOCK, 16, D), lambda b: (0, b // 4, 0))
    smem = pl.BlockSpec(memory_space=pltpu.SMEM)
    return pl.pallas_call(
        far_kernel,
        grid=(count,),
        in_specs=[
            smem,
            smem,
            of_query(0, HEADS, BLOCK, 2 * BLOCK),
            whole(count + 4, BLOCK, 2 * D),
            fours,
            whole(VIRT, 2 * D),
            whole(D, 2 * D),
            whole(2 * D, D),
        ],
        out_specs=[
            fours,
            of_query(0, HEADS, KEYS, 2 * BLOCK),
            of_query(0, KEYS, 2 * D),
            of_query(0, HEADS, BLOCK),
        ],
        out_shape=[
            jax.ShapeDtypeStruct((BLOCK, listed, D), BF),
            jax.ShapeDtypeStruct((count, HEADS, KEYS, 2 * BLOCK), BF),
            jax.ShapeDtypeStruct((count, KEYS, 2 * D), BF),
            jax.ShapeDtypeStruct((count, HEADS, BLOCK), F32),
        ],
        scratch_shapes=[
            pltpu.VMEM((16, BLOCK, D), BF),
            pltpu.VMEM((EXPD * BLOCK, 2 * D), BF),
            pltpu.VMEM((KEYS, BLOCK), BF),
            pltpu.VMEM((BLOCK, 2 * BLOCK), BF),
            pltpu.VMEM((2, KEYS, BLOCK), F32),
            pltpu.VMEM((2, KEYS, BLOCK), BF),
            pltpu.VMEM((2, 8, BLOCK), F32),
        ],
        compiler_params=params(46),
        cost_estimate=cost(count * 6_500_000_000, count * 7_000_000),
        name="far_part",
    )(rel, live, sides, kvx, far, vkv, wkv, wkvt)


def near_kernel(
    rel_ref, sides_ref, pairs_ref, kv_ref, inverse_ref, wo_ref, mixed_ref, dq_ref, near_ref, near_grads, att, dqt
):
    b = pl.program_id(0)

    @pl.when(b == 0)
    def _():
        near_ref[...] = jnp.zeros_like(near_ref)

    for h in range(HEADS):
        rows = slice(h * HEAD, (h + 1) * HEAD)
        sums = dot(kv_ref[0, :, head_cols(h)], pairs_ref[0, h], TN)
        inverse = inverse_ref[0, h : h + 1, :]
        dqt[rows, :] = sums[:HEAD, :BLOCK] * inverse
        att[rows, :] = sums[HEAD:, BLOCK:] * inverse
        side = scaled(sides_ref[0, h], inverse)
        near_grads[:, head_cols(h)] = dot(pairs_ref[0, h, :NEAR, :], side, NT)
    for s in range(LOCD):
        near_ref[rel_ref[b, s]] += near_grads[s * BLOCK : (s + 1) * BLOCK, :]
    mixed_ref[0] = dot(att[...].T.astype(BF), wo_ref[...]).astype(BF)
    dq_ref[0] = (dqt[...] * HEAD**-0.5).T.astype(BF)


def near_part(rel, sides, pairs, kv, inverse, wo):
    count = rel.shape[0]
    return pl.pallas_call(
        near_kernel,
        grid=(count,),
        in_specs=[
            pl.BlockSpec(memory_space=pltpu.SMEM),
            of_query(0, HEADS, BLOCK, 2 * BLOCK),
            of_query(0, HEADS, KEYS, 2 * BLOCK),
            of_query(0, KEYS, 2 * D),
            of_query(0, HEADS, BLOCK),
            whole(D, D),
        ],
        out_specs=[
            of_query(0, BLOCK, D),
            of_query(0, BLOCK, D),
            kept(count + 4, BLOCK, 2 * D),
        ],
        out_shape=[
            jax.ShapeDtypeStruct((count, BLOCK, D), BF),
            jax.ShapeDtypeStruct((count, BLOCK, D), BF),
            jax.ShapeDtypeStruct((count + 4, BLOCK, 2 * D), F32),
        ],
        scratch_shapes=[
            pltpu.VMEM((NEAR, 2 * D), F32),
            pltpu.VMEM((D, BLOCK), F32),
            pltpu.VMEM((D, BLOCK), F32),
        ],
        compiler_params=params(34),
        cost_estimate=cost(count * 3_500_000_000, count * 7_000_000),
        name="near_part",
    )(rel, sides, pairs, kv, inverse, wo)


def exchange(rows):
    return lax.all_to_all(rows, AXES, split_axis=0, concat_axis=0, tiled=True)


def beside(low, high):
    up = [(i, i + 1) for i in range(NDEV - 1)]
    down = [(j, i) for i, j in up]
    return lax.ppermute(high, AXES, up), lax.ppermute(low, AXES, down)


def on_device(
    node_features,
    virtual_features,
    w_qkv,
    output_weight,
    block_home,
    local_blocks,
    expander_blocks,
    key_live,
    out_grad,
):
    me = lax.axis_index(AXES)
    x = node_features.reshape(BLK_DEV, BLOCK, D)
    grads = out_grad.reshape(BLK_DEV, BLOCK, D)
    striped = stripe(x)
    stripes = exchange(striped.reshape(NDEV, FOLD, WIDE)).reshape(NDEV * FOLD, WIDE)

    w_kv = w_qkv[:, D:].reshape(D, 2, HEADS, HEAD).transpose(0, 2, 1, 3).reshape(D, 2 * D)
    w_kvt = w_kv.T
    w_qt = w_qkv[:, :D].T
    vkv = dot(virtual_features, w_kv).astype(BF)

    graph = jnp.arange(NB, dtype=jnp.int32)

    def stored_at(ids, home):
        same = ids[..., None] == graph
        return jnp.sum(jnp.where(same, home, 0), axis=-1, dtype=jnp.int32)

    near_at = stored_at(local_blocks, block_home)
    rel = near_at - (me * BLK_DEV - 2)
    owner, inner = block_home // BLK_DEV, block_home % BLK_DEV
    code = jnp.where(inner < FOLD, owner * FOLD + inner, SPLIT + owner * 4 + inner - FOLD)
    far_codes = stored_at(expander_blocks.reshape(NDEV, BLK_DEV * EXPD), code)
    low_x, high_x, far_codes = lax.optimization_barrier((x[:2], x[BLK_DEV - 2 :], far_codes))
    before, after = beside(low_x, high_x)
    codes = [far_codes[:, EXPD * f : EXPD * (f + n)].reshape(-1) for f, n in PARTS]
    tall = spread(codes[0])
    stripes, before, after, w_kv, w_kvt, w_qt, vkv, rel, tall, codes = lax.optimization_barrier(
        (stripes, before, after, w_kv, w_kvt, w_qt, vkv, rel, tall, codes)
    )

    rows = pick_rows(tall, stripes)
    incoming = exchange(rows.reshape(NDEV, -1, D))
    later = pick_rows(spread(codes[1]), stripes)
    x_ext = jnp.concatenate([before, x, after], axis=0)

    def prepared(first, count):
        kvx = project(x_ext, w_kv, first, count + 4)
        return kvx, make_sides(x, grads, w_qt, output_weight, first, count)

    ready = prepared(*PARTS[0])
    incoming, later, ready, x_ext = lax.optimization_barrier((incoming, later, ready, x_ext))
    incoming = [incoming, exchange(later.reshape(NDEV, -1, D))]

    mixed, d_query, near, back = [], [], [], []
    for c, (first, count) in enumerate(PARTS):
        own = rel[first : first + count] - first
        live = key_live[first : first + count]
        kvx, sides = ready
        far_back, pairs, kv, inverse = far_part(
            own, live, sides, kvx, incoming[c], vkv, w_kv, w_kvt
        )
        back.append(exchange(far_back).reshape(-1, D))
        m, dq, na = near_part(own, sides, pairs, kv, inverse, output_weight)
        if c == 0:
            ready = prepared(*PARTS[1])
            incoming[1], m, dq, na, ready = lax.optimization_barrier(
                (incoming[1], m, dq, na, ready)
            )
        mixed.append(m)
        d_query.append(dq)
        near.append(na)

    acc = add_rows(codes[0][None, :], back[0])
    low, high = beside(near[0][:2].astype(BF), near[-1][-2:].astype(BF))
    low, high, acc, back[1] = lax.optimization_barrier((low, high, acc, back[1]))
    sums = []
    for c, (first, count) in enumerate(PARTS):
        total = near[c][2 : 2 + count]
        prior = low.astype(F32) if c == 0 else near[c - 1][-2:]
        nextp = high.astype(F32) if c == len(PARTS) - 1 else near[c + 1][:2]
        rest = jnp.zeros((count - 4, BLOCK, 2 * D), F32)
        sums.append(total + jnp.concatenate([prior, rest, nextp], axis=0))
    near_sum = jnp.concatenate(sums, axis=0).astype(BF).reshape(BLK_DEV * BLOCK, 2 * D)
    d_q = jnp.concatenate(d_query, axis=0).reshape(BLK_DEV * BLOCK, D)
    base = dot(d_q, w_qt) + dot(near_sum, w_kvt)

    far_sum = last_add_rows(codes[1][None, :], back[1], acc)
    far = exchange(far_sum.reshape(NDEV, FOLD, WIDE)).reshape(NDEV * FOLD, WIDE)
    node_grad = finish(base.reshape(BLK_DEV, BLOCK, D), far)
    mixed = jnp.concatenate(mixed, axis=0).reshape(BLK_DEV * BLOCK, D)
    return mixed, node_grad.reshape(BLK_DEV * BLOCK, D)


def solution(mesh):
    rows = P(AXES, None)
    return jax.shard_map(
        on_device,
        mesh=mesh,
        in_specs=(rows, P(), P(), P(), P(), rows, P(), rows, rows),
        out_specs=(rows, rows),
        check_vma=False,
    )
```
